128 devices in a mesh: lon: 16 (over x, y_hi, core), lat: 8 (over z, y_lo).
Axes of the slice: x: 4, y: 4 (y_hi: 2, y_lo: 2; y = y_hi * 2 + y_lo), z: 4, core: 2. Of those that a mesh axis runs over, the one named last changes fastest.
Arguments:
- features: bfloat16 [32768, 4096], P(('lon', 'lat')), may hold values from 0.0099487305 to 1
- cosine_zenith: bfloat16 [32768], P(('lon', 'lat')), may hold values from 0.049804688 to 1
- albedo: bfloat16 [2, 32768], P(None, ('lon', 'lat')), may hold values from 0.049804688 to 0.84765625
- sunlit: int32 [32768], P(('lon', 'lat')), may hold values 0 or 1
- column_map: int32 [32768], P(('lon', 'lat')), may hold values from -1 to 16383, as said below
- swap_list: int32 [8192], P(('lon', 'lat')), may hold values from 0 to 127, as said below
- gas_table: bfloat16 [64, 224], replicated, may hold values from 0 to 5
- asymmetry: float32 [112], replicated, may hold values from 0 to 0.8
- solar_source: float32 [112], replicated, may hold values from 0.5 to 2
Outputs:
- absorbed: float32 [64, 32768], P(None, ('lon', 'lat'))
- group_mean: float32 [128, 64], P(('lon', 'lat'))
The draws below stay inside these ranges and needn't reach their ends.
Inputs may be any that keep to these rules, and one draw needn't show every extreme that they name: `column_map`: A value t names place t of the groups (group t // 128, slot t % 128); -1 marks an empty owner slot. Every place is named exactly once. The slots of one owner device name at most 4 places of one group, and in every draw some owner names exactly 4 places of some group; in every draw some owner device has all 256 slots live. `swap_list`: entries k * 64 to (k + 1) * 64 - 1 are 64 distinct slots of group k.
All inputs are finite; a program needn't handle non-finite values. No bound on the sum of `sunlit` on one device may be relied on, other than what follows from the above.
Results may differ from the reference program's by a relative error of at most 0.0003.
Values may be sent and summed in bfloat16 or wider, within the bound.
A program may use at most 128 MiB of HBM per device.

```python
import math
import jax
import jax.numpy as jnp
from jax import lax

G = 112
LEV = 64
NF = 64
COL_DEV = 128
GROUPS = 128
HALF = 64
SLOTS = 32768
COLUMNS = 16384


def draw_column_map(key, part):
    key = jax.random.fold_in(key, 5)
    k_off, k_send, k_recv, k_take, k_pair, k_full = jax.random.split(key, 6)
    count = GROUPS
    repeat = COL_DEV // GROUPS
    others = 2 + jax.random.permutation(k_off, count - 2)
    mult = jnp.full((count,), repeat, jnp.int32).at[0].set(2 * repeat).at[1].set(2 * repeat)
    mult = mult.at[others[:count // 4 - 2]].add(repeat)
    mult = mult.at[others[count // 4 - 2:count // 2 - 2]].add(-repeat)
    offset_of = jnp.repeat(jnp.arange(count, dtype=jnp.int32), mult, total_repeat_length=COL_DEV)
    taken_perm = 2 + jax.random.permutation(k_take, count - 2)
    taken = jnp.zeros((count,), jnp.int32).at[0].set(1).at[1].set(1)
    taken = taken.at[taken_perm[:count // 2 - 2]].set(1)
    heavy_bit = jax.random.randint(k_pair, (count // 2,), 0, 2)
    full_pair = jax.random.randint(k_full, (), 0, count // 2)
    owners = jnp.arange(count, dtype=jnp.int32)
    pair_of = owners // 2
    is_heavy = owners % 2 == heavy_bit[pair_of]
    mate = owners ^ 1
    send_perm = jax.vmap(lambda kk: jax.random.permutation(kk, 2 * COL_DEV))(jax.random.split(k_send, count))
    recv_perm = jax.vmap(lambda kk: jax.random.permutation(kk, COL_DEV))(jax.random.split(k_recv, count))
    table_idx = jnp.arange(COL_DEV, dtype=jnp.int32)
    offsets = offset_of[None, :]
    moves = (~is_heavy)[:, None] & ((taken[offsets] == 1) | (pair_of == full_pair)[:, None])
    real_owner = jnp.where(moves, mate[:, None], owners[:, None])
    position = jnp.where(moves, COL_DEV + table_idx[None, :], table_idx[None, :])
    final_pos = send_perm[real_owner, position]
    target_group = (owners[:, None] + offsets) % count
    target = target_group * COL_DEV + recv_perm[target_group, table_idx[None, :]]
    flat_index = (real_owner * (2 * COL_DEV) + final_pos).reshape(-1)
    return jnp.full((SLOTS,), -1, jnp.int32).at[flat_index].set(target.reshape(-1).astype(jnp.int32))


def draw_swap_list(key, part):
    key = jax.random.fold_in(key, 9)
    perms = jax.vmap(lambda kk: jax.random.permutation(kk, COL_DEV))(jax.random.split(key, GROUPS))
    return perms[:, :HALF].reshape(-1).astype(jnp.int32)


def draw_gas_table(key, part):
    key = jax.random.fold_in(key, 13)
    k_abs, k_ray, k_entries = jax.random.split(key, 3)
    rough = jnp.exp(jax.random.uniform(k_entries, (NF, 2 * G), jnp.float32, math.log(0.2), math.log(5.0)))
    low_abs = 0.05
    high_abs = 20.0
    total_abs = jnp.exp(jax.random.uniform(k_abs, (G,), jnp.float32, math.log(low_abs), math.log(high_abs)))
    total_ray = jnp.exp(jax.random.uniform(k_ray, (G,), jnp.float32, math.log(0.02), math.log(2.0)))
    totals = jnp.concatenate([total_abs, total_ray], axis=0)
    scale = totals / (LEV * NF * 0.32)
    return (rough * scale[None, :]).astype(jnp.bfloat16)


def touch_ends(array, own_key, smallest, largest):
    extent = array.shape
    index_at = [jax.random.randint(jax.random.fold_in(own_key, axis), (), 0, extent[axis]) for axis in range(len(extent))]
    array = array.at[tuple(index_at)].set(smallest)
    longest = extent.index(max(extent))
    index_at[longest] = (index_at[longest] + 1) % extent[longest]
    return array.at[tuple(index_at)].set(largest)


def block_levels(stream_key, dims, cuts, least, largest):
    gain, own = 1.0, jax.random.fold_in(stream_key, 6)
    for axis_at, parts in cuts:
        steps = jnp.exp(jax.random.uniform(jax.random.fold_in(own, axis_at), (parts,), jnp.float32, least / len(cuts), largest / len(cuts)))
        gain = gain * jnp.repeat(steps, dims[axis_at] // parts).reshape([-1 if axis == axis_at else 1 for axis in range(len(dims))])
    return gain


def setup_inputs(seed: int = 0) -> dict:
    key_list = jax.random.split(jax.random.key(seed), 10)
    features = jnp.clip(jnp.exp(math.log(1.0) - 4.61031033 * jax.random.uniform(key_list[0], (SLOTS, LEV * NF), jnp.float32) ** block_levels(key_list[0], (SLOTS, LEV * NF), ((0, 128),), -0.2, 0.2)), 0.0099487305, 1.0).astype(jnp.bfloat16)
    cosine_zenith = jnp.clip(0.049804688 + 0.9501953 * jax.random.uniform(key_list[1], (SLOTS,), jnp.float32) ** block_levels(key_list[1], (SLOTS,), ((0, 128),), -0.2, 0.2), 0.049804688, 1.0).astype(jnp.bfloat16)
    albedo = jnp.clip(0.049804688 + 0.79785156 * jax.random.uniform(key_list[2], (2, SLOTS), jnp.float32) ** block_levels(key_list[2], (2, SLOTS), ((1, 128),), -0.2, 0.2), 0.049804688, 0.84765625).astype(jnp.bfloat16)
    sunlit = touch_ends((jax.random.randint(key_list[3], (SLOTS,), 0, 3) < 2).astype(jnp.int32), jax.random.fold_in(key_list[3], 1), 0, 1)
    column_map = draw_column_map(jax.random.fold_in(key_list[9], 71), 0)
    swap_list = draw_swap_list(jax.random.fold_in(key_list[9], 71), 0)
    gas_table = draw_gas_table(jax.random.fold_in(key_list[9], 71), 0)
    asymmetry = jnp.clip(jax.random.uniform(key_list[7], (G,), jnp.float32, 0.0, 0.8), 0.0, 0.8)
    solar_source = jnp.clip(jnp.exp(jax.random.uniform(key_list[8], (G,), jnp.float32, math.log(0.5), math.log(2.0))), 0.5, 2.0)
    return dict(features=features, cosine_zenith=cosine_zenith, albedo=albedo, sunlit=sunlit, column_map=column_map, swap_list=swap_list, gas_table=gas_table, asymmetry=asymmetry, solar_source=solar_source)


def column_fluxes(tau_abs, tau_ray, asym, source, surface):
    cosine = surface[0]
    alb_dir = surface[1]
    alb_dif = surface[2]
    daylit = surface[3]
    depth = tau_abs + tau_ray
    single = 0.98 * tau_ray / depth
    asy = asym[None, :, None]
    gamma_one = (8.0 - single * (5.0 + 3.0 * asy)) * 0.25
    gamma_two = 0.75 * single * (1.0 - asy)
    eigen = jnp.sqrt((gamma_one - gamma_two) * (gamma_one + gamma_two))
    decay_one = jnp.exp(-eigen * depth)
    decay_two = decay_one * decay_one
    inverse_den = 1.0 / (eigen * (1.0 + decay_two) + gamma_one * (1.0 - decay_two))
    refl_dif = gamma_two * (1.0 - decay_two) * inverse_den
    tran_dif = 2.0 * eigen * decay_one * inverse_den
    direct_tran = jnp.exp(-depth / cosine[None, None, :])
    scattered = single * (1.0 - direct_tran)
    backward = 0.5 - 0.25 * asy
    refl_dir = scattered * backward
    tran_dir = scattered * (1.0 - backward)
    incoming = source[:, None] * (cosine * daylit)[None, :]

    def down_direct(flux, trans):
        return (flux * trans, flux)
    bottom, dir_top = lax.scan(down_direct, incoming, direct_tran)
    src_up = refl_dir * dir_top
    src_dn = tran_dir * dir_top

    def upward(carry, layer):
        alb_below, src_below = carry
        rd, td, su, sd = layer
        denominator = 1.0 / (1.0 - rd * alb_below)
        new_alb = rd + td * td * alb_below * denominator
        new_src = su + td * denominator * (src_below + alb_below * sd)
        return ((new_alb, new_src), (alb_below, src_below, denominator))
    start_alb = jnp.broadcast_to(alb_dif[None, :], incoming.shape)
    start_src = alb_dir[None, :] * bottom
    (alb_top, src_top), (alb_stack, src_stack, den_stack) = lax.scan(upward, (start_alb, start_src), (refl_dif, tran_dif, src_up, src_dn), reverse=True)

    def downward(flux_dn, layer):
        rd, td, sd, ab, sb, de = layer
        next_dn = (td * flux_dn + rd * sb + sd) * de
        next_up = ab * next_dn + sb
        return (next_dn, next_dn - next_up)
    _, diffuse_net = lax.scan(downward, jnp.zeros_like(incoming), (refl_dif, tran_dif, src_dn, alb_stack, src_stack, den_stack))
    dir_below = jnp.concatenate([dir_top[1:], bottom[None]], axis=0)
    net_below = dir_below + diffuse_net
    net_first = incoming - src_top
    net_above = jnp.concatenate([net_first[None], net_below[:-1]], axis=0)
    return lax.optimization_barrier(jnp.sum(net_above - net_below, axis=1))

def group_absorbed(feat, surface, gas_table, asymmetry, solar_source):
    rows = feat.shape[0]
    feat_three = feat.reshape(rows, LEV, NF).astype(jnp.float32)
    depth = jnp.einsum('blf,fh->lhb', feat_three, gas_table.astype(jnp.float32), precision=lax.Precision.HIGHEST)
    return column_fluxes(depth[:, :G], depth[:, G:], asymmetry, solar_source, surface)

def reference(features, cosine_zenith, albedo, sunlit, column_map, swap_list, gas_table, asymmetry, solar_source):
    safe_map = jnp.where(column_map >= 0, column_map, COLUMNS).astype(jnp.int32)
    inverse = jnp.zeros((COLUMNS,), jnp.int32).at[safe_map].set(jnp.arange(SLOTS, dtype=jnp.int32), mode='drop')
    lists = swap_list.reshape(GROUPS, HALF)
    group_ids = jnp.arange(GROUPS, dtype=jnp.int32)
    partner = ((group_ids + GROUPS // 2) % GROUPS).astype(jnp.int32)
    place = (group_ids[:, None] * COL_DEV + lists).reshape(-1)
    content = (partner[:, None] * COL_DEV + lists[partner]).reshape(-1)
    held = jnp.arange(COLUMNS, dtype=jnp.int32).at[place].set(content)
    source_slot = inverse[held].reshape(GROUPS, COL_DEV)
    surface_all = jnp.stack([cosine_zenith, albedo[0], albedo[1], sunlit.astype(jnp.bfloat16)], axis=0)

    def one_group(slots):
        feat = features[slots]
        surface = surface_all[:, slots].astype(jnp.float32)
        return group_absorbed(feat, surface, gas_table, asymmetry, solar_source)
    per_group = lax.map(one_group, source_slot)
    group_mean = lax.optimization_barrier(jnp.mean(per_group, axis=2))
    rows = jnp.transpose(per_group, (0, 2, 1)).reshape(COLUMNS, LEV)
    absorbed = jnp.zeros((SLOTS, LEV), jnp.float32).at[source_slot.reshape(-1)].set(rows)
    return (absorbed.T, group_mean)
```

```python
import functools
import jax
import jax.numpy as jnp
from jax import lax
from jax.sharding import PartitionSpec as P
from jax.experimental import pallas as pl
from jax.experimental.pallas import tpu as pltpu

LEV = 64
NF = 64
G = 112
LANES = 128
SUB = 8
GB = G // SUB
PAIRS = LEV // 2
LOG2E = 1.4426950408889634


def recip(x):
    return pl.reciprocal(x, approx=True)


def column_kernel(
    feat_ref, cosine_ref, albedo_ref, sunlit_ref, map_ref, gas_ref, asym_ref, solar_ref,
    out_ref,
    weight_ref, depth_ref, const_ref, state_ref, gain_ref, add_ref, admit_ref, down_ref, net_ref,
):
    f32 = jnp.float32
    bf16 = jnp.bfloat16

    table = gas_ref[...]
    stacked = jnp.concatenate([table, table], axis=0)
    row = lax.broadcasted_iota(jnp.int32, (2 * G, 2 * G), 0)
    col = lax.broadcasted_iota(jnp.int32, (2 * G, 2 * G), 1)
    unit = jnp.where(row == col, 1.0, 0.0).astype(bf16)
    turned = lax.dot_general(unit, stacked, (((1,), (1,)), ((), ())), preferred_element_type=f32)
    tau_rows = 2.0 * (turned[:G] + turned[G:])
    ray_rows = (2.0 * 0.98) * turned[G:]
    lane = lax.broadcasted_iota(jnp.int32, (G, LANES), 1)
    for part, value in enumerate((tau_rows, ray_rows)):
        high = value.astype(bf16).astype(f32)
        low = value - high
        for parity in range(2):
            keep = (lane < NF) if parity == 0 else (lane >= NF)
            at = (2 * parity + part) * G
            weight_ref[at : at + G, :LANES] = jnp.where(keep, high, 0.0).astype(bf16)
            weight_ref[at : at + G, LANES:] = jnp.where(keep, low, 0.0).astype(bf16)

    def to_rows(line):
        wide = jnp.broadcast_to(line, (LANES, G))
        return wide.T

    asym = to_rows(asym_ref[...])
    solar = to_rows(solar_ref[...])
    const_ref[0] = 0.25 * (1.0 + 3.0 * asym)
    const_ref[1] = 0.5 - 0.25 * asym

    cosine = cosine_ref[...].astype(f32)
    day = sunlit_ref[...].astype(f32)
    slant = jnp.broadcast_to(-0.5 * LOG2E / cosine, (SUB, LANES))
    state_ref[0] = solar * (cosine * day)
    state_ref[1] = jnp.ones((G, LANES), f32)
    state_ref[2] = jnp.zeros((G, LANES), f32)
    state_ref[3] = jnp.zeros((G, LANES), f32)

    def optical(pair, slot):
        chunk = feat_ref[:, pl.ds(pl.multiple_of(pair * LANES, LANES), LANES)]
        twice = jnp.concatenate([chunk, chunk], axis=1)
        depth_ref[slot] = lax.dot_general(
            weight_ref[...], twice, (((1,), (1,)), ((), ())), preferred_element_type=f32
        )

    optical(0, 0)

    def down(pair, carry):
        slot = lax.rem(pair, 2)
        optical(jnp.minimum(pair + 1, PAIRS - 1), 1 - slot)
        totals = [jnp.zeros((SUB, LANES), f32) for _ in range(2)]
        for g in range(GB):
            rows = pl.ds(g * SUB, SUB)
            direct, admit, source, left = (state_ref[n, rows, :] for n in range(4))
            slope = const_ref[0, rows, :]
            back = const_ref[1, rows, :]
            for odd in range(2):
                layer = 2 * pair + odd
                tau = depth_ref[slot, pl.ds(2 * odd * G + g * SUB, SUB), :]
                ray = depth_ref[slot, pl.ds((2 * odd + 1) * G + g * SUB, SUB), :]
                single = ray * recip(tau)
                f_one = 1.0 - single
                f_two = 1.0 - single * slope
                root = lax.rsqrt(f_one * f_two)
                sigma = f_one * root
                x = f_two * sigma * tau
                th = jnp.tanh(x)
                e = jnp.exp2(x * (-LOG2E))
                sech = e + e * th
                trans = jnp.exp2(tau * slant)
                below = direct * trans
                scattered = single * (direct - below)
                up = back * scattered
                dn = scattered - up
                jump = up - left
                totals[odd] = totals[odd] + (source + direct)
                inner = source + up - admit * jump
                z = recip(sigma + admit * th)
                zs = z * sigma
                gain = sech * zs
                gain_ref[layer, rows, :] = gain
                add_ref[layer, rows, :] = (th * z) * inner + jump
                admit_ref[layer, rows, :] = admit
                admit = (admit + sigma * th) * zs
                source = gain * inner + dn
                direct = below
                left = dn
            for n, value in enumerate((direct, admit, source, left)):
                state_ref[n, rows, :] = value
        for odd in range(2):
            down_ref[2 * pair + odd] = totals[odd]
        return carry

    lax.fori_loop(0, PAIRS, down, 0)

    alb_dir = jnp.broadcast_to(albedo_ref[0:1, :].astype(f32), (SUB, LANES))
    alb_dif = jnp.broadcast_to(albedo_ref[1:2, :].astype(f32), (SUB, LANES))
    fluxes = []
    total = jnp.zeros((SUB, LANES), f32)
    for g in range(GB):
        rows = pl.ds(g * SUB, SUB)
        direct, admit, source, left = (state_ref[n, rows, :] for n in range(4))
        over = source * (1.0 + alb_dif) + 2.0 * alb_dir * direct - left * (1.0 - alb_dif)
        flux = over / ((1.0 - alb_dif) + admit * (1.0 + alb_dif))
        total = total + (direct + source - admit * flux)
        fluxes.append(flux)
    net_ref[LEV : LEV + 1, :] = jnp.sum(total, axis=0, keepdims=True)

    def upward(step, carry):
        layer = LEV - 1 - step
        total = down_ref[layer]
        out = []
        for g in range(GB):
            rows = pl.ds(g * SUB, SUB)
            flux = gain_ref[layer, rows, :] * carry[g] + add_ref[layer, rows, :]
            total = total - admit_ref[layer, rows, :] * flux
            out.append(flux)
        net_ref[pl.ds(layer, 1), :] = jnp.sum(total, axis=0, keepdims=True)
        return tuple(out)

    lax.fori_loop(0, LEV, upward, tuple(fluxes))
    live = map_ref[...] >= 0
    absorbed = net_ref[0:LEV, :] - net_ref[1 : LEV + 1, :]
    out_ref[...] = jnp.where(live, absorbed, 0.0)


def columns_absorbed(features, cosine, albedo, sunlit, column_map, gas_table, asymmetry, solar):
    count = features.shape[0]
    blocks = count // LANES
    line = lambda n: pl.BlockSpec((n, LANES), lambda i: (0, i))
    whole = lambda shape: pl.BlockSpec(shape, lambda i: (0,) * len(shape))
    return pl.pallas_call(
        column_kernel,
        grid=(blocks,),
        out_shape=jax.ShapeDtypeStruct((LEV, count), jnp.float32),
        in_specs=[
            pl.BlockSpec((LANES, LEV * NF), lambda i: (i, 0)),
            line(1), line(2), line(1), line(1),
            whole((NF, 2 * G)), whole((1, G)), whole((1, G)),
        ],
        out_specs=pl.BlockSpec((LEV, LANES), lambda i: (0, i)),
        scratch_shapes=[
            pltpu.VMEM((4 * G, 2 * LANES), jnp.bfloat16),
            pltpu.VMEM((2, 4 * G, LANES), jnp.float32),
            pltpu.VMEM((2, G, LANES), jnp.float32),
            pltpu.VMEM((4, G, LANES), jnp.float32),
            pltpu.VMEM((LEV, G, LANES), jnp.float32),
            pltpu.VMEM((LEV, G, LANES), jnp.float32),
            pltpu.VMEM((LEV, G, LANES), jnp.float32),
            pltpu.VMEM((LEV, SUB, LANES), jnp.float32),
            pltpu.VMEM((LEV + SUB, LANES), jnp.float32),
        ],
        compiler_params=pltpu.CompilerParams(vmem_limit_bytes=32 * 1024 * 1024),
        cost_estimate=pl.CostEstimate(flops=200_000_000, bytes_accessed=2_200_000, transcendentals=10_000_000),
    )(features, cosine[None], albedo, sunlit[None], column_map[None], gas_table, asymmetry[None], solar[None])


def group_means(absorbed, column_map, swap_list):
    axes = ("lon", "lat")
    groups = lax.axis_size("lon") * lax.axis_size("lat")
    slots = jnp.arange(LANES, dtype=jnp.int32)
    lists = lax.all_gather(swap_list, axes, axis=0, tiled=False)
    swapped = jnp.any(lists[:, :, None] == slots[None, None, :], axis=1)
    home = column_map // LANES
    place = column_map % LANES
    moved = swapped[jnp.maximum(home, 0), place]
    held = jnp.where(moved, (home + groups // 2) % groups, home)
    held = jnp.where(column_map >= 0, held, -1)
    member = (held[None, :] == jnp.arange(groups, dtype=jnp.int32)[:, None]).astype(jnp.float32)
    sums = lax.dot_general(
        member, absorbed, (((1,), (1,)), ((), ())), precision=lax.Precision.HIGHEST
    )
    mine = lax.psum_scatter(sums, axes, scatter_dimension=0, tiled=True)
    return mine * (1.0 / LANES)


def body(
    features, cosine_zenith, albedo, sunlit, column_map, swap_list, gas_table, asymmetry, solar_source
):
    absorbed = columns_absorbed(
        features, cosine_zenith, albedo, sunlit, column_map, gas_table, asymmetry, solar_source
    )
    return absorbed, group_means(absorbed, column_map, swap_list)


def solution(mesh):
    both = ("lon", "lat")
    in_specs = (
        P(both, None), P(both), P(None, both), P(both), P(both), P(both), P(), P(), P(),
    )
    out_specs = (P(None, both), P(both, None))
    return jax.shard_map(body, mesh=mesh, in_specs=in_specs, out_specs=out_specs, check_vma=False)
```

```python
import functools
import jax
import jax.numpy as jnp
from jax import lax
from jax.sharding import PartitionSpec as P
from jax.experimental import pallas as pl
from jax.experimental.pallas import tpu as pltpu

LEV = 64
NF = 64
G = 112
HALF_G = G // 2
LANES = 128
SUB = 8
GB = HALF_G // SUB
PAIRS = LEV // 2
SLOTS = 256
BLOCK = 64
KINDS = 5
LOG2E = 1.4426950408889634
NT = (((1,), (1,)), ((), ()))
NN = (((1,), (0,)), ((), ()))


def recip(x):
    return pl.reciprocal(x, approx=True)


def mxu(a, b, dims):
    return lax.dot_general(a, b, dims, preferred_element_type=jnp.float32)


def column_kernel(
    feat_hbm, cosine_hbm, albedo_hbm, sunlit_hbm, map_hbm, gas_hbm, asym_hbm, solar_hbm,
    out_ref,
    feat_ref, cosine_ref, albedo_ref, sunlit_ref, map_ref, gas_ref, asym_ref, solar_ref,
    packed_ref, weight_ref, spread_ref, surface_ref, solar_rows_ref, depth_a, depth_b, depth_c, depth_d,
    state_ref, gain_ref, add_ref, admit_ref, down_ref, net_ref, small_sem, feat_sem,
):
    f32 = jnp.float32
    bf16 = jnp.bfloat16
    chunks = [
        pltpu.make_async_copy(
            feat_hbm.at[:, pl.ds(n * 1024, 1024)], feat_ref.at[:, pl.ds(n * 1024, 1024)], feat_sem.at[n]
        )
        for n in range(4)
    ]
    small = [
        pltpu.make_async_copy(src, dst, small_sem.at[n])
        for n, (src, dst) in enumerate(
            (
                (sunlit_hbm, sunlit_ref), (map_hbm, map_ref), (cosine_hbm, cosine_ref),
                (albedo_hbm, albedo_ref), (gas_hbm, gas_ref), (asym_hbm, asym_ref), (solar_hbm, solar_ref),
            )
        )
    ]
    for copy in small:
        copy.start()
    for copy in chunks:
        copy.start()
    for copy in small:
        copy.wait()

    day = sunlit_ref[...].astype(f32)
    lit = jnp.where((map_ref[...] >= 0) & (sunlit_ref[...] != 0), 1.0, 0.0)
    count = jnp.sum(lit).astype(jnp.int32)
    row = lax.broadcasted_iota(jnp.int32, (SLOTS, SLOTS), 0)
    col = lax.broadcasted_iota(jnp.int32, (SLOTS, SLOTS), 1)
    upper = jnp.where(row <= col, 1.0, 0.0).astype(bf16)
    rank = mxu(jnp.broadcast_to(lit, (SUB, SLOTS)).astype(bf16), upper, NN)[0:1]
    rank = jnp.where(lit > 0.0, rank, 0.0).astype(jnp.int32) - 1
    pick = jnp.where(rank == row, 1.0, 0.0).astype(bf16)
    for n in range(SLOTS // BLOCK):
        part = pick[n * BLOCK : (n + 1) * BLOCK]
        spread_ref[n, :BLOCK, :] = part
        spread_ref[n, BLOCK:, :] = part
    faces = jnp.concatenate(
        [cosine_ref[...].astype(f32), albedo_ref[...].astype(f32), day, jnp.zeros((4, SLOTS), f32)], axis=0
    ).astype(bf16)
    for n in range(SLOTS // BLOCK):
        surface_ref[n] = mxu(faces, spread_ref[n], NT)

    table = gas_ref[...]
    stacked = jnp.concatenate([table, table], axis=0)
    unit = jnp.where(row == col, 1.0, 0.0)[: 2 * G, : 2 * G].astype(bf16)
    turned = mxu(unit, stacked, NT)
    first = lax.broadcasted_iota(jnp.int32, (HALF_G, LANES), 1) < BLOCK

    def halves(rows, at):
        return jnp.where(first, rows[at : at + HALF_G], rows[at + HALF_G : at + G])

    def to_rows(line):
        return halves(jnp.broadcast_to(line, (LANES, G)).T, 0)

    asym = to_rows(asym_ref[...])
    solar_rows_ref[...] = to_rows(solar_ref[...])
    absorb = halves(turned, 0)
    scatter = halves(turned, G)
    quantities = (
        absorb + scatter,
        2.0 * absorb + (2.0 - 2.0 * 0.98) * scatter,
        2.0 * absorb + (2.0 - 0.49 * (1.0 + 3.0 * asym)) * scatter,
        0.98 * (0.5 - 0.25 * asym) * scatter,
        0.98 * (0.5 + 0.25 * asym) * scatter,
    )
    for n, value in enumerate(quantities):
        high = value.astype(bf16)
        weight_ref[n * HALF_G : (n + 1) * HALF_G, :LANES] = high
        weight_ref[n * HALF_G : (n + 1) * HALF_G, LANES:] = (value - high.astype(f32)).astype(bf16)

    for n in range(4):
        chunks[n].wait()

        def pack(step, carry):
            at = pl.ds(pl.multiple_of(n * 1024 + step * 256, 256), 256)
            packed_ref[:, at] = mxu(pick, feat_ref[:, at], NN).astype(bf16)
            return carry

        lax.fori_loop(0, 4, pack, 0)

    out_ref[...] = jnp.zeros((LEV, SLOTS), f32)
    low_lanes = lax.broadcasted_iota(jnp.int32, (BLOCK, LANES), 1) < BLOCK
    nothing = jnp.zeros((BLOCK, LANES), bf16)

    def one_block(block, carry):
        faces_here = surface_ref[block]
        lane = lax.broadcasted_iota(jnp.int32, (1, LANES), 1)
        within = jnp.where(lane >= BLOCK, lane - BLOCK, lane) + block * BLOCK < count
        cosine = jnp.where(within, faces_here[0:1], 1.0)
        slant = jnp.broadcast_to(-LOG2E / cosine, (SUB, LANES))
        alb_dir = jnp.broadcast_to(faces_here[1:2], (SUB, LANES))
        alb_dif = jnp.broadcast_to(faces_here[2:3], (SUB, LANES))
        state_ref[0] = solar_rows_ref[...] * (cosine * faces_here[3:4])
        state_ref[1] = jnp.ones((HALF_G, LANES), f32)
        state_ref[2] = jnp.zeros((HALF_G, LANES), f32)
        state_ref[3] = jnp.zeros((HALF_G, LANES), f32)

        def optical(pair, depth):
            chunk = packed_ref[
                pl.ds(pl.multiple_of(block * BLOCK, BLOCK), BLOCK),
                pl.ds(pl.multiple_of(pair * LANES, LANES), LANES),
            ]
            turn = jnp.concatenate([chunk[:, BLOCK:], chunk[:, :BLOCK]], axis=1)
            both = jnp.concatenate(
                [
                    jnp.where(low_lanes, chunk, nothing),
                    jnp.where(low_lanes, nothing, turn),
                    jnp.where(low_lanes, turn, nothing),
                    jnp.where(low_lanes, nothing, chunk),
                ],
                axis=0,
            )
            depth[...] = mxu(weight_ref[...], jnp.concatenate([both, both], axis=1), NT)

        def one_pair(pair, depth):
            totals = [jnp.zeros((SUB, LANES), f32) for _ in range(2)]
            for g in range(GB):
                rows = pl.ds(g * SUB, SUB)
                direct, admit, source, left = (state_ref[n, rows, :] for n in range(4))
                for odd in range(2):
                    layer = 2 * pair + odd
                    tau, t_one, t_two, to_up, to_dn = (
                        depth[n * HALF_G + g * SUB : n * HALF_G + (g + 1) * SUB, odd * LANES : (odd + 1) * LANES]
                        for n in range(KINDS)
                    )
                    product = t_one * t_two
                    root = lax.rsqrt(product)
                    x = product * root
                    sigma = t_one * root
                    th = jnp.tanh(x)
                    e = jnp.exp2(x * (-LOG2E))
                    sech = e + e * th
                    below = direct * jnp.exp2(tau * slant)
                    lost = (direct - below) * recip(tau)
                    up = to_up * lost
                    dn = to_dn * lost
                    jump = up - left
                    totals[odd] = totals[odd] + (source + direct)
                    inner = source + up - admit * jump
                    z = recip(sigma + admit * th)
                    zs = z * sigma
                    gain = sech * zs
                    gain_ref[layer, rows, :] = gain
                    add_ref[layer, rows, :] = (th * z) * inner + jump
                    admit_ref[layer, rows, :] = admit
                    admit = (admit + sigma * th) * zs
                    source = gain * inner + dn
                    direct = below
                    left = dn
                for n, value in enumerate((direct, admit, source, left)):
                    state_ref[n, rows, :] = value
            for odd in range(2):
                down_ref[2 * pair + odd] = totals[odd]

        optical(0, depth_a)
        optical(1, depth_b)

        def down(step, inner_carry):
            @pl.when(count > 0)
            def _():
                one_pair(4 * step, depth_a)
                one_pair(4 * step + 1, depth_b)
                optical(4 * step + 2, depth_c)
                optical(4 * step + 3, depth_d)

            @pl.when(count > 0)
            def _():
                one_pair(4 * step + 2, depth_c)
                one_pair(4 * step + 3, depth_d)
                optical(jnp.minimum(4 * step + 4, PAIRS - 2), depth_a)
                optical(jnp.minimum(4 * step + 5, PAIRS - 1), depth_b)

            return inner_carry

        lax.fori_loop(0, PAIRS // 4, down, 0)

        fluxes = []
        total = jnp.zeros((SUB, LANES), f32)
        for g in range(GB):
            rows = pl.ds(g * SUB, SUB)
            direct, admit, source, left = (state_ref[n, rows, :] for n in range(4))
            over = source * (1.0 + alb_dif) + 2.0 * alb_dir * direct - left * (1.0 - alb_dif)
            flux = over / ((1.0 - alb_dif) + admit * (1.0 + alb_dif))
            total = total + (direct + source - admit * flux)
            fluxes.append(flux)
        net_ref[LEV : LEV + 1, :] = jnp.sum(total, axis=0, keepdims=True)

        def upward(step, fluxes):
            for odd in range(4):
                layer = LEV - 1 - 4 * step - odd
                total = down_ref[layer]
                out = []
                for g in range(GB):
                    rows = pl.ds(g * SUB, SUB)
                    flux = gain_ref[layer, rows, :] * fluxes[g] + add_ref[layer, rows, :]
                    total = total - admit_ref[layer, rows, :] * flux
                    out.append(flux)
                fluxes = tuple(out)
                net_ref[pl.ds(layer, 1), :] = jnp.sum(total, axis=0, keepdims=True)
            return fluxes

        lax.fori_loop(0, LEV // 4, upward, tuple(fluxes))
        absorbed = jnp.where(within, net_ref[0:LEV, :] - net_ref[1 : LEV + 1, :], 0.0)
        high = absorbed.astype(bf16)
        low = (absorbed - high.astype(f32)).astype(bf16)
        home = spread_ref[block]
        out_ref[...] += mxu(high, home, NN) + mxu(low, home, NN)
        return carry

    lax.fori_loop(0, lax.div(count + (BLOCK - 1), BLOCK), one_block, 0)


def columns_absorbed(features, cosine, albedo, sunlit, column_map, gas_table, asymmetry, solar):
    anywhere = pl.BlockSpec(memory_space=pl.ANY)
    f32, bf16, i32 = jnp.float32, jnp.bfloat16, jnp.int32
    return pl.pallas_call(
        column_kernel,
        out_shape=jax.ShapeDtypeStruct((LEV, SLOTS), f32),
        in_specs=[anywhere] * 8,
        out_specs=pl.BlockSpec(memory_space=pltpu.VMEM),
        scratch_shapes=[
            pltpu.VMEM((SLOTS, LEV * NF), bf16),
            pltpu.VMEM((1, SLOTS), bf16),
            pltpu.VMEM((2, SLOTS), bf16),
            pltpu.VMEM((1, SLOTS), i32),
            pltpu.VMEM((1, SLOTS), i32),
            pltpu.VMEM((NF, 2 * G), bf16),
            pltpu.VMEM((1, G), f32),
            pltpu.VMEM((1, G), f32),
            pltpu.VMEM((SLOTS, LEV * NF), bf16),
            pltpu.VMEM((KINDS * HALF_G, 2 * LANES), bf16),
            pltpu.VMEM((SLOTS // BLOCK, LANES, SLOTS), bf16),
            pltpu.VMEM((SLOTS // BLOCK, SUB, LANES), f32),
            pltpu.VMEM((HALF_G, LANES), f32),
            pltpu.VMEM((KINDS * HALF_G, 2 * LANES), f32),
            pltpu.VMEM((KINDS * HALF_G, 2 * LANES), f32),
            pltpu.VMEM((KINDS * HALF_G, 2 * LANES), f32),
            pltpu.VMEM((KINDS * HALF_G, 2 * LANES), f32),
            pltpu.VMEM((4, HALF_G, LANES), f32),
            pltpu.VMEM((LEV, HALF_G, LANES), f32),
            pltpu.VMEM((LEV, HALF_G, LANES), f32),
            pltpu.VMEM((LEV, HALF_G, LANES), f32),
            pltpu.VMEM((LEV, SUB, LANES), f32),
            pltpu.VMEM((LEV + SUB, LANES), f32),
            pltpu.SemaphoreType.DMA((7,)),
            pltpu.SemaphoreType.DMA((4,)),
        ],
        compiler_params=pltpu.CompilerParams(vmem_limit_bytes=60 * 1024 * 1024),
        cost_estimate=pl.CostEstimate(flops=200_000_000, bytes_accessed=2_200_000, transcendentals=10_000_000),
    )(features, cosine[None], albedo, sunlit[None], column_map[None], gas_table, asymmetry[None], solar[None])


def mean_kernel(absorbed_ref, map_ref, swap_ref, mean_ref, own_ref, row_ref, mask_ref, part_ref, first_ref, strip_ref, second_ref, send_a, recv_a, send_b, recv_b, send_c, recv_c, send_d, recv_d):
    f32 = jnp.float32
    bf16 = jnp.bfloat16
    n_lon, n_lat = lax.axis_size("lon"), lax.axis_size("lat")
    lon, lat = lax.axis_index("lon"), lax.axis_index("lat")
    groups = n_lon * n_lat
    lon_peers = [lax.rem(lon + d, n_lon) for d in range(n_lon)]
    lat_peers = [lax.rem(lat + d, n_lat) for d in range(n_lat)]

    barrier = pltpu.get_barrier_semaphore()
    for d in range(1, n_lat):
        pl.semaphore_signal(barrier, inc=1, device_id=(lon, lat_peers[d]), device_id_type=pl.DeviceIdType.MESH)
    for d in range(1, n_lon):
        pl.semaphore_signal(barrier, inc=1, device_id=(lon_peers[d], lat), device_id_type=pl.DeviceIdType.MESH)

    listed = jnp.broadcast_to(swap_ref[...].astype(f32), (LANES, LANES // 2)).T
    lane = lax.broadcasted_iota(jnp.int32, (LANES // 2, LANES), 1).astype(f32)
    mine = jnp.max(jnp.where(listed == lane, 1.0, 0.0), axis=0, keepdims=True)
    own_ref[0] = mine
    row_ref[lat] = mine
    pl.semaphore_wait(barrier, n_lat + n_lon - 2)

    def send(src, dst, sends, recvs, d, device):
        copy = pltpu.make_async_remote_copy(
            src_ref=src, dst_ref=dst, send_sem=sends.at[d], recv_sem=recvs.at[d],
            device_id=device, device_id_type=pl.DeviceIdType.MESH,
        )
        copy.start()
        return copy

    along_lat = lambda d: (lon, lat_peers[d])
    along_lon = lambda d: (lon_peers[d], lat)
    copies = [send(own_ref.at[0], row_ref.at[lat], send_a, recv_a, d, along_lat(d)) for d in range(1, n_lat)]
    for copy in copies:
        copy.wait()
    mask_ref[lon] = row_ref[...]
    copies = [send(row_ref, mask_ref.at[lon], send_b, recv_b, d, along_lon(d)) for d in range(1, n_lon)]

    place = map_ref[...]
    home = lax.shift_right_arithmetic(place, 7)
    slot = place & (LANES - 1)
    row = lax.broadcasted_iota(jnp.int32, (groups, SLOTS), 0)
    at_home = jnp.where(home == row, 1.0, 0.0).astype(bf16)
    at_slot = jnp.where(slot == lax.broadcasted_iota(jnp.int32, (LANES, SLOTS), 0), 1.0, 0.0)
    absorbed = absorbed_ref[...]
    absorbed = jnp.concatenate([absorbed, jnp.zeros((LANES - LEV, SLOTS), f32)], axis=0)
    high = absorbed.astype(bf16)
    low = (absorbed - high.astype(f32)).astype(bf16)
    for copy in copies:
        copy.wait()

    masks = mask_ref[...].reshape(groups, LANES)
    listed_at = mxu(masks.T.astype(bf16), at_home, NN)
    moved = jnp.sum(listed_at * at_slot, axis=0, keepdims=True)
    away = jnp.where(home >= groups // 2, home - groups // 2, home + groups // 2)
    held = jnp.where(place < 0, -1, jnp.where(moved > 0.5, away, home))
    member = jnp.where(held == row, 1.0, 0.0).astype(bf16)
    sums = mxu(member, high, NT) + mxu(member, low, NT)
    part_ref[...] = sums.reshape(n_lon, n_lat, LANES)

    copies = [send(part_ref.at[lon_peers[d]], first_ref.at[d], send_c, recv_c, d, along_lon(d)) for d in range(1, n_lon)]
    total = part_ref[lon]
    for d, copy in enumerate(copies):
        copy.wait()
    for d in range(1, n_lon):
        total = total + first_ref[d]
    for n in range(n_lat):
        strip_ref[n] = total[n : n + 1]

    copies = [send(strip_ref.at[lat_peers[d]], second_ref.at[d], send_d, recv_d, d, along_lat(d)) for d in range(1, n_lat)]
    total = strip_ref[lat]
    for copy in copies:
        copy.wait()
    for d in range(1, n_lat):
        total = total + second_ref[d]
    mean_ref[...] = total[:, :LEV] * (1.0 / LANES)


def group_means(absorbed, column_map, swap_list):
    n_lon, n_lat = lax.axis_size("lon"), lax.axis_size("lat")
    f32 = jnp.float32
    vmem = pl.BlockSpec(memory_space=pltpu.VMEM)
    dma = pltpu.SemaphoreType.DMA
    return pl.pallas_call(
        mean_kernel,
        out_shape=jax.ShapeDtypeStruct((1, LEV), f32),
        in_specs=[vmem] * 3,
        out_specs=vmem,
        scratch_shapes=[
            pltpu.VMEM((1, 1, LANES), f32),
            pltpu.VMEM((n_lat, 1, LANES), f32),
            pltpu.VMEM((n_lon, n_lat, 1, LANES), f32),
            pltpu.VMEM((n_lon, n_lat, LANES), f32),
            pltpu.VMEM((n_lon, n_lat, LANES), f32),
            pltpu.VMEM((n_lat, 1, LANES), f32),
            pltpu.VMEM((n_lat, 1, LANES), f32),
            dma((n_lat,)), dma((n_lat,)), dma((n_lon,)), dma((n_lon,)),
            dma((n_lon,)), dma((n_lon,)), dma((n_lat,)), dma((n_lat,)),
        ],
        compiler_params=pltpu.CompilerParams(collective_id=0, has_side_effects=True, vmem_limit_bytes=60 * 1024 * 1024),
        cost_estimate=pl.CostEstimate(flops=20_000_000, bytes_accessed=200_000, transcendentals=0),
    )(absorbed, column_map[None], swap_list[None])


def body(
    features, cosine_zenith, albedo, sunlit, column_map, swap_list, gas_table, asymmetry, solar_source
):
    absorbed = columns_absorbed(
        features, cosine_zenith, albedo, sunlit, column_map, gas_table, asymmetry, solar_source
    )
    return absorbed, group_means(absorbed, column_map, swap_list)


def solution(mesh):
    both = ("lon", "lat")
    in_specs = (
        P(both, None), P(both), P(None, both), P(both), P(both), P(both), P(), P(), P(),
    )
    out_specs = (P(None, both), P(both, None))
    return jax.shard_map(body, mesh=mesh, in_specs=in_specs, out_specs=out_specs, check_vma=False)
```

```python
import functools
import jax
import jax.numpy as jnp
from jax import lax
from jax.sharding import PartitionSpec as P
from jax.experimental import pallas as pl
from jax.experimental.pallas import tpu as pltpu

LEV = 64
NF = 64
G = 112
HALF_G = G // 2
LANES = 128
SUB = 8
GB = HALF_G // SUB
PAIRS = LEV // 2
SLOTS = 256
BLOCK = 64
KINDS = 5
LOG2E = 1.4426950408889634
NT = (((1,), (1,)), ((), ()))
NN = (((1,), (0,)), ((), ()))


def recip(x):
    return pl.reciprocal(x, approx=True)


def mxu(a, b, dims):
    return lax.dot_general(a, b, dims, preferred_element_type=jnp.float32)


def column_kernel(
    feat_hbm, cosine_hbm, albedo_hbm, sunlit_hbm, map_hbm, gas_hbm, asym_hbm, solar_hbm, swap_hbm,
    out_ref, mean_ref,
    feat_ref, cosine_ref, albedo_ref, sunlit_ref, map_ref, gas_ref, asym_ref, solar_ref, swap_ref,
    packed_ref, weight_ref, spread_ref, surface_ref, solar_rows_ref, depth_a, depth_b, depth_c, depth_d,
    state_ref, gain_ref, add_ref, admit_ref, down_ref, net_ref, own_ref, mask_ref, part_ref, other_ref, strip_ref, last_ref,
    small_sem, feat_sem, send_a, recv_a, send_b, recv_b, send_c, recv_c,
):
    f32 = jnp.float32
    bf16 = jnp.bfloat16
    chunks = [
        pltpu.make_async_copy(
            feat_hbm.at[:, pl.ds(n * 1024, 1024)], feat_ref.at[:, pl.ds(n * 1024, 1024)], feat_sem.at[n]
        )
        for n in range(4)
    ]
    small = [
        pltpu.make_async_copy(src, dst, small_sem.at[n])
        for n, (src, dst) in enumerate(
            (
                (sunlit_hbm, sunlit_ref), (map_hbm, map_ref), (cosine_hbm, cosine_ref),
                (albedo_hbm, albedo_ref), (gas_hbm, gas_ref), (asym_hbm, asym_ref), (solar_hbm, solar_ref),
                (swap_hbm, swap_ref),
            )
        )
    ]
    for copy in small:
        copy.start()
    for copy in chunks:
        copy.start()

    n_lon, n_lat = lax.axis_size("lon"), lax.axis_size("lat")
    lon, lat = lax.axis_index("lon"), lax.axis_index("lat")
    groups = n_lon * n_lat
    chips = groups // 2
    core = lax.rem(lon, 2)
    chip = lax.div(lon, 2) * n_lat + lat
    mesh_ids = pl.DeviceIdType.MESH
    sibling = (lon + 1 - 2 * core, lat)
    peers = [
        (lax.rem(lon + 2 * a, n_lon), lax.rem(lat + c, n_lat))
        for a in range(n_lon // 2) for c in range(n_lat) if a or c
    ]
    barrier = pltpu.get_barrier_semaphore()
    for device in [sibling] + peers:
        pl.semaphore_signal(barrier, inc=1, device_id=device, device_id_type=mesh_ids)

    def remote(src, dst, sends, recvs, n, device):
        copy = pltpu.make_async_remote_copy(
            src_ref=src, dst_ref=dst, send_sem=sends.at[n], recv_sem=recvs.at[n],
            device_id=device, device_id_type=mesh_ids,
        )
        copy.start()
        return copy

    for copy in small:
        copy.wait()

    listed = jnp.broadcast_to(swap_ref[...].astype(f32), (LANES, LANES // 2)).T
    lane_no = lax.broadcasted_iota(jnp.int32, (LANES // 2, LANES), 1).astype(f32)
    own_ref[0] = jnp.max(jnp.where(listed == lane_no, 1.0, 0.0), axis=0, keepdims=True)

    day = sunlit_ref[...].astype(f32)
    lit = jnp.where((map_ref[...] >= 0) & (sunlit_ref[...] != 0), 1.0, 0.0)
    count = jnp.sum(lit).astype(jnp.int32)
    row = lax.broadcasted_iota(jnp.int32, (SLOTS, SLOTS), 0)
    col = lax.broadcasted_iota(jnp.int32, (SLOTS, SLOTS), 1)
    upper = jnp.where(row <= col, 1.0, 0.0).astype(bf16)
    rank = mxu(jnp.broadcast_to(lit, (SUB, SLOTS)).astype(bf16), upper, NN)[0:1]
    rank = jnp.where(lit > 0.0, rank, 0.0).astype(jnp.int32) - 1
    pick = jnp.where(rank == row, 1.0, 0.0).astype(bf16)
    for n in range(SLOTS // BLOCK):
        part = pick[n * BLOCK : (n + 1) * BLOCK]
        spread_ref[n, :BLOCK, :] = part
        spread_ref[n, BLOCK:, :] = part
    faces = jnp.concatenate(
        [cosine_ref[...].astype(f32), albedo_ref[...].astype(f32), day, jnp.zeros((4, SLOTS), f32)], axis=0
    ).astype(bf16)
    for n in range(SLOTS // BLOCK):
        surface_ref[n] = mxu(faces, spread_ref[n], NT)

    table = gas_ref[...]
    stacked = jnp.concatenate([table, table], axis=0)
    unit = jnp.where(row == col, 1.0, 0.0)[: 2 * G, : 2 * G].astype(bf16)
    turned = mxu(unit, stacked, NT)
    first = lax.broadcasted_iota(jnp.int32, (HALF_G, LANES), 1) < BLOCK

    def halves(rows, at):
        return jnp.where(first, rows[at : at + HALF_G], rows[at + HALF_G : at + G])

    def to_rows(line):
        return halves(jnp.broadcast_to(line, (LANES, G)).T, 0)

    asym = to_rows(asym_ref[...])
    solar_rows_ref[...] = to_rows(solar_ref[...])
    absorb = halves(turned, 0)
    scatter = halves(turned, G)
    quantities = (
        absorb + scatter,
        2.0 * absorb + (2.0 - 2.0 * 0.98) * scatter,
        2.0 * absorb + (2.0 - 0.49 * (1.0 + 3.0 * asym)) * scatter,
        0.98 * (0.5 - 0.25 * asym) * scatter,
        0.98 * (0.5 + 0.25 * asym) * scatter,
    )
    for n, value in enumerate(quantities):
        high = value.astype(bf16)
        weight_ref[n * HALF_G : (n + 1) * HALF_G, :LANES] = high
        weight_ref[n * HALF_G : (n + 1) * HALF_G, LANES:] = (value - high.astype(f32)).astype(bf16)

    for n in range(4):
        chunks[n].wait()

        def pack(step, carry):
            at = pl.ds(pl.multiple_of(n * 1024 + step * 256, 256), 256)
            packed_ref[:, at] = mxu(pick, feat_ref[:, at], NN).astype(bf16)
            return carry

        lax.fori_loop(0, 4, pack, 0)

    out_ref[...] = jnp.zeros((LEV, SLOTS), f32)
    low_lanes = lax.broadcasted_iota(jnp.int32, (BLOCK, LANES), 1) < BLOCK
    nothing = jnp.zeros((BLOCK, LANES), bf16)

    def one_block(block, carry):
        faces_here = surface_ref[block]
        lane = lax.broadcasted_iota(jnp.int32, (1, LANES), 1)
        within = jnp.where(lane >= BLOCK, lane - BLOCK, lane) + block * BLOCK < count
        cosine = jnp.where(within, faces_here[0:1], 1.0)
        slant = jnp.broadcast_to(-LOG2E / cosine, (SUB, LANES))
        alb_dir = jnp.broadcast_to(faces_here[1:2], (SUB, LANES))
        alb_dif = jnp.broadcast_to(faces_here[2:3], (SUB, LANES))
        state_ref[0] = solar_rows_ref[...] * (cosine * faces_here[3:4])
        state_ref[1] = jnp.ones((HALF_G, LANES), f32)
        state_ref[2] = jnp.zeros((HALF_G, LANES), f32)
        state_ref[3] = jnp.zeros((HALF_G, LANES), f32)

        def optical(pair, depth):
            chunk = packed_ref[
                pl.ds(pl.multiple_of(block * BLOCK, BLOCK), BLOCK),
                pl.ds(pl.multiple_of(pair * LANES, LANES), LANES),
            ]
            turn = jnp.concatenate([chunk[:, BLOCK:], chunk[:, :BLOCK]], axis=1)
            both = jnp.concatenate(
                [
                    jnp.where(low_lanes, chunk, nothing),
                    jnp.where(low_lanes, nothing, turn),
                    jnp.where(low_lanes, turn, nothing),
                    jnp.where(low_lanes, nothing, chunk),
                ],
                axis=0,
            )
            depth[...] = mxu(weight_ref[...], jnp.concatenate([both, both], axis=1), NT)

        def one_pair(pair, depth):
            totals = [jnp.zeros((SUB, LANES), f32) for _ in range(2)]
            for g in range(GB):
                rows = pl.ds(g * SUB, SUB)
                direct, admit, source, left = (state_ref[n, rows, :] for n in range(4))
                for odd in range(2):
                    layer = 2 * pair + odd
                    tau, t_one, t_two, to_up, to_dn = (
                        depth[n * HALF_G + g * SUB : n * HALF_G + (g + 1) * SUB, odd * LANES : (odd + 1) * LANES]
                        for n in range(KINDS)
                    )
                    product = t_one * t_two
                    root = lax.rsqrt(product)
                    x = product * root
                    sigma = t_one * root
                    th = jnp.tanh(x)
                    e = jnp.exp2(x * (-LOG2E))
                    sech = e + e * th
                    below = direct * jnp.exp2(tau * slant)
                    lost = (direct - below) * recip(tau)
                    up = to_up * lost
                    dn = to_dn * lost
                    jump = up - left
                    totals[odd] = totals[odd] + (source + direct)
                    inner = source + up - admit * jump
                    z = recip(sigma + admit * th)
                    zs = z * sigma
                    gain = sech * zs
                    gain_ref[layer, rows, :] = gain
                    add_ref[layer, rows, :] = (th * z) * inner + jump
                    admit_ref[layer, rows, :] = admit
                    admit = (admit + sigma * th) * zs
                    source = gain * inner + dn
                    direct = below
                    left = dn
                for n, value in enumerate((direct, admit, source, left)):
                    state_ref[n, rows, :] = value
            for odd in range(2):
                down_ref[2 * pair + odd] = totals[odd]

        optical(0, depth_a)
        optical(1, depth_b)

        def down(step, inner_carry):
            one_pair(4 * step, depth_a)
            one_pair(4 * step + 1, depth_b)
            optical(4 * step + 2, depth_c)
            optical(4 * step + 3, depth_d)
            one_pair(4 * step + 2, depth_c)
            one_pair(4 * step + 3, depth_d)
            optical(jnp.minimum(4 * step + 4, PAIRS - 2), depth_a)
            optical(jnp.minimum(4 * step + 5, PAIRS - 1), depth_b)
            return inner_carry

        lax.fori_loop(0, PAIRS // 4, down, 0)

        fluxes = []
        total = jnp.zeros((SUB, LANES), f32)
        for g in range(GB):
            rows = pl.ds(g * SUB, SUB)
            direct, admit, source, left = (state_ref[n, rows, :] for n in range(4))
            over = source * (1.0 + alb_dif) + 2.0 * alb_dir * direct - left * (1.0 - alb_dif)
            flux = over / ((1.0 - alb_dif) + admit * (1.0 + alb_dif))
            total = total + (direct + source - admit * flux)
            fluxes.append(flux)
        net_ref[LEV : LEV + 1, :] = jnp.sum(total, axis=0, keepdims=True)

        def upward(step, fluxes):
            for odd in range(4):
                layer = LEV - 1 - 4 * step - odd
                total = down_ref[layer]
                out = []
                for g in range(GB):
                    rows = pl.ds(g * SUB, SUB)
                    flux = gain_ref[layer, rows, :] * fluxes[g] + add_ref[layer, rows, :]
                    total = total - admit_ref[layer, rows, :] * flux
                    out.append(flux)
                fluxes = tuple(out)
                net_ref[pl.ds(layer, 1), :] = jnp.sum(total, axis=0, keepdims=True)
            return fluxes

        lax.fori_loop(0, LEV // 4, upward, tuple(fluxes))
        absorbed = jnp.where(within, net_ref[0:LEV, :] - net_ref[1 : LEV + 1, :], 0.0)
        high = absorbed.astype(bf16)
        low = (absorbed - high.astype(f32)).astype(bf16)
        home = spread_ref[block]
        out_ref[...] += mxu(high, home, NN) + mxu(low, home, NN)
        return carry

    lax.fori_loop(0, 1, one_block, 0)

    pl.semaphore_wait(barrier, chips)
    mask_ref[core, chip] = own_ref[0]
    copies = [
        remote(own_ref.at[0], mask_ref.at[core, chip], send_a, recv_a, n, device)
        for n, device in enumerate(peers)
    ]
    lax.fori_loop(1, 2, one_block, 0)
    for copy in copies:
        copy.wait()
    copy = remote(mask_ref.at[core], mask_ref.at[core], send_b, recv_b, 0, sibling)
    lax.fori_loop(2, 4, one_block, 0)
    copy.wait()

    place = map_ref[...]
    home = lax.shift_right_arithmetic(place, 7)
    home_core = lax.rem(lax.div(home, n_lat), 2)
    home_chip = lax.div(home, 2 * n_lat) * n_lat + lax.rem(home, n_lat)
    away_chip = jnp.where(home_chip >= chips // 2, home_chip - chips // 2, home_chip + chips // 2)
    slot = place & (LANES - 1)
    group_row = lax.broadcasted_iota(jnp.int32, (groups, SLOTS), 0)
    at_home = jnp.where(home_core * chips + home_chip == group_row, 1.0, 0.0).astype(bf16)
    at_slot = jnp.where(slot == lax.broadcasted_iota(jnp.int32, (LANES, SLOTS), 0), 1.0, 0.0)
    masks = mask_ref[...].reshape(groups, LANES)
    listed_at = mxu(masks.T.astype(bf16), at_home, NN)
    moved = jnp.sum(listed_at * at_slot, axis=0, keepdims=True)
    held = home_core * chips + jnp.where(moved > 0.5, away_chip, home_chip)
    held = jnp.where(place < 0, -1, held)
    member = jnp.where(held == group_row, 1.0, 0.0).astype(bf16)
    absorbed = jnp.concatenate([out_ref[...], jnp.zeros((LANES - LEV, SLOTS), f32)], axis=0)
    high = absorbed.astype(bf16)
    low = (absorbed - high.astype(f32)).astype(bf16)
    part_ref[...] = (mxu(member, high, NT) + mxu(member, low, NT)).reshape(2, chips, LANES)

    copy = remote(part_ref.at[1 - core], other_ref, send_b, recv_b, 1, sibling)
    copy.wait()
    strip_ref[...] = (part_ref[core] + other_ref[...]).reshape(chips, 1, LANES)
    copies = [
        remote(strip_ref.at[lax.div(device[0], 2) * n_lat + device[1]], last_ref.at[n], send_c, recv_c, n, device)
        for n, device in enumerate(peers)
    ]
    for copy in copies:
        copy.wait()
    total = strip_ref[chip] + jnp.sum(last_ref[...], axis=0)
    mean_ref[...] = total[:, :LEV] * (1.0 / LANES)


def columns_absorbed(features, cosine, albedo, sunlit, column_map, swap_list, gas_table, asymmetry, solar):
    anywhere = pl.BlockSpec(memory_space=pl.ANY)
    vmem = pl.BlockSpec(memory_space=pltpu.VMEM)
    f32, bf16, i32 = jnp.float32, jnp.bfloat16, jnp.int32
    n_lon, n_lat = lax.axis_size("lon"), lax.axis_size("lat")
    chips = n_lon * n_lat // 2
    dma = pltpu.SemaphoreType.DMA
    return pl.pallas_call(
        column_kernel,
        out_shape=(jax.ShapeDtypeStruct((LEV, SLOTS), f32), jax.ShapeDtypeStruct((1, LEV), f32)),
        in_specs=[anywhere] * 9,
        out_specs=(vmem, vmem),
        scratch_shapes=[
            pltpu.VMEM((SLOTS, LEV * NF), bf16),
            pltpu.VMEM((1, SLOTS), bf16),
            pltpu.VMEM((2, SLOTS), bf16),
            pltpu.VMEM((1, SLOTS), i32),
            pltpu.VMEM((1, SLOTS), i32),
            pltpu.VMEM((NF, 2 * G), bf16),
            pltpu.VMEM((1, G), f32),
            pltpu.VMEM((1, G), f32),
            pltpu.VMEM((1, LANES // 2), i32),
            pltpu.VMEM((SLOTS, LEV * NF), bf16),
            pltpu.VMEM((KINDS * HALF_G, 2 * LANES), bf16),
            pltpu.VMEM((SLOTS // BLOCK, LANES, SLOTS), bf16),
            pltpu.VMEM((SLOTS // BLOCK, SUB, LANES), f32),
            pltpu.VMEM((HALF_G, LANES), f32),
            pltpu.VMEM((KINDS * HALF_G, 2 * LANES), f32),
            pltpu.VMEM((KINDS * HALF_G, 2 * LANES), f32),
            pltpu.VMEM((KINDS * HALF_G, 2 * LANES), f32),
            pltpu.VMEM((KINDS * HALF_G, 2 * LANES), f32),
            pltpu.VMEM((4, HALF_G, LANES), f32),
            pltpu.VMEM((LEV, HALF_G, LANES), f32),
            pltpu.VMEM((LEV, HALF_G, LANES), f32),
            pltpu.VMEM((LEV, HALF_G, LANES), f32),
            pltpu.VMEM((LEV, SUB, LANES), f32),
            pltpu.VMEM((LEV + SUB, LANES), f32),
            pltpu.VMEM((1, 1, LANES), f32),
            pltpu.VMEM((2, chips, 1, LANES), f32),
            pltpu.VMEM((2, chips, LANES), f32),
            pltpu.VMEM((chips, LANES), f32),
            pltpu.VMEM((chips, 1, LANES), f32),
            pltpu.VMEM((chips - 1, 1, LANES), f32),
            dma((8,)), dma((4,)), dma((chips,)), dma((chips,)), dma((2,)), dma((2,)), dma((chips,)), dma((chips,)),
        ],
        compiler_params=pltpu.CompilerParams(collective_id=0, has_side_effects=True, vmem_limit_bytes=60 * 1024 * 1024),
        cost_estimate=pl.CostEstimate(flops=200_000_000, bytes_accessed=2_200_000, transcendentals=10_000_000),
    )(features, cosine[None], albedo, sunlit[None], column_map[None], gas_table, asymmetry[None], solar[None], swap_list[None])


def body(
    features, cosine_zenith, albedo, sunlit, column_map, swap_list, gas_table, asymmetry, solar_source
):
    return columns_absorbed(
        features, cosine_zenith, albedo, sunlit, column_map, swap_list, gas_table, asymmetry, solar_source
    )


def solution(mesh):
    both = ("lon", "lat")
    in_specs = (
        P(both, None), P(both), P(None, both), P(both), P(both), P(both), P(), P(), P(),
    )
    out_specs = (P(None, both), P(both, None))
    return jax.shard_map(body, mesh=mesh, in_specs=in_specs, out_specs=out_specs, check_vma=False)
```

```python
import functools
import jax
import jax.numpy as jnp
from jax import lax
from jax.sharding import PartitionSpec as P
from jax.experimental import pallas as pl
from jax.experimental.pallas import tpu as pltpu

LEV = 64
NF = 64
G = 112
LANES = 128
SUB = 8
GB = G // SUB
PAIRS = LEV // 2
KINDS = 2
LOG2E = 1.4426950408889634
NT = (((1,), (1,)), ((), ()))
NN = (((1,), (0,)), ((), ()))


def recip(x):
    return pl.reciprocal(x, approx=True)


def mxu(a, b, dims):
    return lax.dot_general(a, b, dims, preferred_element_type=jnp.float32)


def column_kernel(
    feat_hbm, cosine_hbm, albedo_hbm, sunlit_hbm, map_hbm, gas_hbm, asym_hbm, solar_hbm, swap_hbm,
    out_ref, mean_ref,
    feat_ref, cosine_ref, albedo_ref, sunlit_ref, map_ref, gas_ref, asym_ref, solar_ref, swap_ref,
    weight_ref, const_ref, solar_rows_ref, depth_0, depth_1, depth_2, depth_3, depth_4, depth_5, depth_6, depth_7,
    state_ref, gain_ref, add_ref, admit_ref, down_ref, net_ref,
    own_ref, mask_ref, part_ref, other_ref, strip_ref, last_ref,
    small_sem, feat_sem, send_a, recv_a, send_b, recv_b, send_c, recv_c,
):
    f32 = jnp.float32
    bf16 = jnp.bfloat16
    chunks = [
        pltpu.make_async_copy(
            feat_hbm.at[pl.ds(n * LANES, LANES), :], feat_ref.at[pl.ds(n * LANES, LANES), :], feat_sem.at[n]
        )
        for n in range(2)
    ]
    small = [
        pltpu.make_async_copy(src, dst, small_sem.at[n])
        for n, (src, dst) in enumerate(
            (
                (sunlit_hbm, sunlit_ref), (map_hbm, map_ref), (cosine_hbm, cosine_ref),
                (albedo_hbm, albedo_ref), (gas_hbm, gas_ref), (asym_hbm, asym_ref), (solar_hbm, solar_ref),
                (swap_hbm, swap_ref),
            )
        )
    ]
    for copy in small:
        copy.start()
    for copy in chunks:
        copy.start()

    n_lon, n_lat = lax.axis_size("lon"), lax.axis_size("lat")
    lon, lat = lax.axis_index("lon"), lax.axis_index("lat")
    groups = n_lon * n_lat
    chips = groups // 2
    core = lax.rem(lon, 2)
    chip = lax.div(lon, 2) * n_lat + lat
    mesh_ids = pl.DeviceIdType.MESH
    sibling = (lon + 1 - 2 * core, lat)
    peers = [
        (lax.rem(lon + 2 * a, n_lon), lax.rem(lat + c, n_lat))
        for a in range(n_lon // 2) for c in range(n_lat) if a or c
    ]
    barrier = pltpu.get_barrier_semaphore()
    for device in [sibling] + peers:
        pl.semaphore_signal(barrier, inc=1, device_id=device, device_id_type=mesh_ids)

    def remote(src, dst, sends, recvs, n, device):
        return pltpu.make_async_remote_copy(
            src_ref=src, dst_ref=dst, send_sem=sends.at[n], recv_sem=recvs.at[n],
            device_id=device, device_id_type=mesh_ids,
        )

    mask_copies = [
        remote(own_ref.at[0], mask_ref.at[core, chip], send_a, recv_a, n, device)
        for n, device in enumerate(peers)
    ]
    mask_pair = remote(mask_ref.at[core], mask_ref.at[core], send_b, recv_b, 0, sibling)

    for copy in small:
        copy.wait()

    listed = jnp.broadcast_to(swap_ref[...].astype(f32), (LANES, LANES // 2)).T
    lane_no = lax.broadcasted_iota(jnp.int32, (LANES // 2, LANES), 1).astype(f32)
    own_ref[0] = jnp.max(jnp.where(listed == lane_no, 1.0, 0.0), axis=0, keepdims=True)

    table = gas_ref[...]
    stacked = jnp.concatenate([table, table], axis=0)
    row = lax.broadcasted_iota(jnp.int32, (2 * G, 2 * G), 0)
    col = lax.broadcasted_iota(jnp.int32, (2 * G, 2 * G), 1)
    turned = mxu(jnp.where(row == col, 1.0, 0.0).astype(bf16), stacked, NT)

    def to_rows(line):
        return jnp.broadcast_to(line, (LANES, G)).T

    asym = to_rows(asym_ref[...])
    solar_rows_ref[...] = to_rows(solar_ref[...])
    absorb = turned[:G]
    scatter = turned[G:]
    first = lax.broadcasted_iota(jnp.int32, (G, LANES), 1) < NF
    weight_ref[:G, :] = jnp.where(first, 2.0 * absorb, 2.0 * scatter).astype(bf16)
    weight_ref[G:, :] = jnp.where(first, 0.0, 2.0 * scatter).astype(bf16)
    const_ref[0] = 0.245 * (1.0 + 3.0 * asym)
    const_ref[1] = 0.98 * (0.5 - 0.25 * asym)
    const_ref[2] = 0.98 * (0.5 + 0.25 * asym)

    low_lanes = lax.broadcasted_iota(jnp.int32, (LANES, LANES), 1) < NF

    def one_block(block, carry):
        @pl.when(block == 0)
        def _():
            chunks[0].wait()

        @pl.when(block == 1)
        def _():
            chunks[1].wait()
            pl.semaphore_wait(barrier, chips)
            mask_ref[core, chip] = own_ref[0]
            for copy in mask_copies:
                copy.start()

        lanes = pl.ds(pl.multiple_of(block * LANES, LANES), LANES)
        cosine = cosine_ref[:, lanes].astype(f32)
        slant = jnp.broadcast_to((-0.5 * LOG2E) / cosine, (SUB, LANES))
        alb_dir = jnp.broadcast_to(albedo_ref[0:1, lanes].astype(f32), (SUB, LANES))
        alb_dif = jnp.broadcast_to(albedo_ref[1:2, lanes].astype(f32), (SUB, LANES))
        state_ref[0] = solar_rows_ref[...] * (cosine * sunlit_ref[:, lanes].astype(f32))
        state_ref[1] = jnp.ones((G, LANES), f32)
        state_ref[2] = jnp.zeros((G, LANES), f32)
        state_ref[3] = jnp.zeros((G, LANES), f32)

        def optical(pair, depth):
            chunk = feat_ref[lanes, pl.ds(pl.multiple_of(pair * LANES, LANES), LANES)]
            turn = jnp.concatenate([chunk[:, NF:], chunk[:, :NF]], axis=1)
            both = jnp.concatenate(
                [jnp.where(low_lanes, chunk, turn), jnp.where(low_lanes, turn, chunk)], axis=0
            )
            depth[...] = mxu(weight_ref[...], both, NT)

        def one_pair(pair, depth):
            totals = [jnp.zeros((SUB, LANES), f32) for _ in range(2)]
            for g in range(GB):
                rows = pl.ds(g * SUB, SUB)
                direct, admit, source, left = (state_ref[n, rows, :] for n in range(4))
                slope, to_up, to_dn = (const_ref[n, rows, :] for n in range(3))
                for odd in range(2):
                    layer = 2 * pair + odd
                    tau, ray = (
                        depth[n * G + g * SUB : n * G + (g + 1) * SUB, odd * LANES : (odd + 1) * LANES]
                        for n in range(KINDS)
                    )
                    t_one = tau - 0.98 * ray
                    t_two = tau - slope * ray
                    product = t_one * t_two
                    root = lax.rsqrt(product)
                    x = product * root
                    sigma = t_one * root
                    th = jnp.tanh(x)
                    e = jnp.exp2(x * (-LOG2E))
                    sech = e + e * th
                    below = direct * jnp.exp2(tau * slant)
                    lost = (direct - below) * recip(tau) * ray
                    up = to_up * lost
                    dn = to_dn * lost
                    jump = up - left
                    totals[odd] = totals[odd] + (source + direct)
                    inner = source + up - admit * jump
                    z = recip(sigma + admit * th)
                    zs = z * sigma
                    gain = sech * zs
                    gain_ref[layer, rows, :] = gain
                    add_ref[layer, rows, :] = (th * z) * inner + jump
                    admit_ref[layer, rows, :] = admit
                    admit = (admit + sigma * th) * zs
                    source = gain * inner + dn
                    direct = below
                    left = dn
                for n, value in enumerate((direct, admit, source, left)):
                    state_ref[n, rows, :] = value
            for odd in range(2):
                down_ref[2 * pair + odd] = totals[odd]

        optical(0, depth_0)
        optical(1, depth_1)
        optical(2, depth_2)
        optical(3, depth_3)

        def down(step, inner_carry):
            one_pair(8 * step + 0, depth_0)
            one_pair(8 * step + 1, depth_1)
            one_pair(8 * step + 2, depth_2)
            one_pair(8 * step + 3, depth_3)
            optical(8 * step + 4, depth_4)
            optical(8 * step + 5, depth_5)
            optical(8 * step + 6, depth_6)
            optical(8 * step + 7, depth_7)
            one_pair(8 * step + 4, depth_4)
            one_pair(8 * step + 5, depth_5)
            one_pair(8 * step + 6, depth_6)
            one_pair(8 * step + 7, depth_7)
            optical(jnp.minimum(8 * step + 8, PAIRS - 1), depth_0)
            optical(jnp.minimum(8 * step + 9, PAIRS - 1), depth_1)
            optical(jnp.minimum(8 * step + 10, PAIRS - 1), depth_2)
            optical(jnp.minimum(8 * step + 11, PAIRS - 1), depth_3)
            return inner_carry

        lax.fori_loop(0, PAIRS // 8, down, 0)

        @pl.when(block == 1)
        def _():
            for copy in mask_copies:
                copy.wait()
            mask_pair.start()

        fluxes = []
        total = jnp.zeros((SUB, LANES), f32)
        for g in range(GB):
            rows = pl.ds(g * SUB, SUB)
            direct, admit, source, left = (state_ref[n, rows, :] for n in range(4))
            over = source * (1.0 + alb_dif) + 2.0 * alb_dir * direct - left * (1.0 - alb_dif)
            flux = over / ((1.0 - alb_dif) + admit * (1.0 + alb_dif))
            total = total + (direct + source - admit * flux)
            fluxes.append(flux)
        net_ref[LEV : LEV + 1, :] = jnp.sum(total, axis=0, keepdims=True)

        def upward(step, fluxes):
            for odd in range(2):
                layer = LEV - 1 - 2 * step - odd
                total = down_ref[layer]
                out = []
                for g in range(GB):
                    rows = pl.ds(g * SUB, SUB)
                    flux = gain_ref[layer, rows, :] * fluxes[g] + add_ref[layer, rows, :]
                    total = total - admit_ref[layer, rows, :] * flux
                    out.append(flux)
                fluxes = tuple(out)
                net_ref[pl.ds(layer, 1), :] = jnp.sum(total, axis=0, keepdims=True)
            return fluxes

        lax.fori_loop(0, LEV // 2, upward, tuple(fluxes))
        live = map_ref[:, lanes] >= 0
        out_ref[:, lanes] = jnp.where(live, net_ref[0:LEV, :] - net_ref[1 : LEV + 1, :], 0.0)
        return carry

    lax.fori_loop(0, 2, one_block, 0)
    mask_pair.wait()

    place = map_ref[...]
    home = lax.shift_right_arithmetic(place, 7)
    home_core = lax.rem(lax.div(home, n_lat), 2)
    home_chip = lax.div(home, 2 * n_lat) * n_lat + lax.rem(home, n_lat)
    away_chip = jnp.where(home_chip >= chips // 2, home_chip - chips // 2, home_chip + chips // 2)
    slot = place & (LANES - 1)
    slots = place.shape[1]
    group_row = lax.broadcasted_iota(jnp.int32, (groups, slots), 0)
    at_home = jnp.where(home_core * chips + home_chip == group_row, 1.0, 0.0).astype(bf16)
    at_slot = jnp.where(slot == lax.broadcasted_iota(jnp.int32, (LANES, slots), 0), 1.0, 0.0)
    masks = mask_ref[...].reshape(groups, LANES)
    listed_at = mxu(masks.T.astype(bf16), at_home, NN)
    moved = jnp.sum(listed_at * at_slot, axis=0, keepdims=True)
    held = home_core * chips + jnp.where(moved > 0.5, away_chip, home_chip)
    held = jnp.where(place < 0, -1, held)
    member = jnp.where(held == group_row, 1.0, 0.0).astype(bf16)
    absorbed = jnp.concatenate([out_ref[...], jnp.zeros((LANES - LEV, slots), f32)], axis=0)
    high = absorbed.astype(bf16)
    low = (absorbed - high.astype(f32)).astype(bf16)
    part_ref[...] = (mxu(member, high, NT) + mxu(member, low, NT)).reshape(2, chips, LANES)

    copy = remote(part_ref.at[1 - core], other_ref, send_b, recv_b, 1, sibling)
    copy.start()
    copy.wait()
    strip_ref[...] = (part_ref[core] + other_ref[...]).reshape(chips, 1, LANES)
    copies = [
        remote(strip_ref.at[lax.div(device[0], 2) * n_lat + device[1]], last_ref.at[n], send_c, recv_c, n, device)
        for n, device in enumerate(peers)
    ]
    for copy in copies:
        copy.start()
    for copy in copies:
        copy.wait()
    total = strip_ref[chip] + jnp.sum(last_ref[...], axis=0)
    mean_ref[...] = total[:, :LEV] * (1.0 / LANES)


def columns_absorbed(features, cosine, albedo, sunlit, column_map, swap_list, gas_table, asymmetry, solar):
    anywhere = pl.BlockSpec(memory_space=pl.ANY)
    vmem = pl.BlockSpec(memory_space=pltpu.VMEM)
    f32, bf16, i32 = jnp.float32, jnp.bfloat16, jnp.int32
    chips = lax.axis_size("lon") * lax.axis_size("lat") // 2
    dma = pltpu.SemaphoreType.DMA
    return pl.pallas_call(
        column_kernel,
        out_shape=(jax.ShapeDtypeStruct((LEV, 2 * LANES), f32), jax.ShapeDtypeStruct((1, LEV), f32)),
        in_specs=[anywhere] * 9,
        out_specs=(vmem, vmem),
        scratch_shapes=[
            pltpu.VMEM((2 * LANES, LEV * NF), bf16),
            pltpu.VMEM((1, 2 * LANES), bf16),
            pltpu.VMEM((2, 2 * LANES), bf16),
            pltpu.VMEM((1, 2 * LANES), i32),
            pltpu.VMEM((1, 2 * LANES), i32),
            pltpu.VMEM((NF, 2 * G), bf16),
            pltpu.VMEM((1, G), f32),
            pltpu.VMEM((1, G), f32),
            pltpu.VMEM((1, LANES // 2), i32),
            pltpu.VMEM((KINDS * G, LANES), bf16),
            pltpu.VMEM((3, G, LANES), f32),
            pltpu.VMEM((G, LANES), f32),
            pltpu.VMEM((KINDS * G, 2 * LANES), f32),
            pltpu.VMEM((KINDS * G, 2 * LANES), f32),
            pltpu.VMEM((KINDS * G, 2 * LANES), f32),
            pltpu.VMEM((KINDS * G, 2 * LANES), f32),
            pltpu.VMEM((KINDS * G, 2 * LANES), f32),
            pltpu.VMEM((KINDS * G, 2 * LANES), f32),
            pltpu.VMEM((KINDS * G, 2 * LANES), f32),
            pltpu.VMEM((KINDS * G, 2 * LANES), f32),
            pltpu.VMEM((4, G, LANES), f32),
            pltpu.VMEM((LEV, G, LANES), f32),
            pltpu.VMEM((LEV, G, LANES), f32),
            pltpu.VMEM((LEV, G, LANES), f32),
            pltpu.VMEM((LEV, SUB, LANES), f32),
            pltpu.VMEM((LEV + SUB, LANES), f32),
            pltpu.VMEM((1, 1, LANES), f32),
            pltpu.VMEM((2, chips, 1, LANES), f32),
            pltpu.VMEM((2, chips, LANES), f32),
            pltpu.VMEM((chips, LANES), f32),
            pltpu.VMEM((chips, 1, LANES), f32),
            pltpu.VMEM((chips - 1, 1, LANES), f32),
            dma((8,)), dma((2,)), dma((chips,)), dma((chips,)), dma((2,)), dma((2,)), dma((chips,)), dma((chips,)),
        ],
        compiler_params=pltpu.CompilerParams(collective_id=0, has_side_effects=True, vmem_limit_bytes=60 * 1024 * 1024),
        cost_estimate=pl.CostEstimate(flops=200_000_000, bytes_accessed=2_200_000, transcendentals=10_000_000),
    )(features, cosine[None], albedo, sunlit[None], column_map[None], gas_table, asymmetry[None], solar[None], swap_list[None])


def body(
    features, cosine_zenith, albedo, sunlit, column_map, swap_list, gas_table, asymmetry, solar_source
):
    return columns_absorbed(
        features, cosine_zenith, albedo, sunlit, column_map, swap_list, gas_table, asymmetry, solar_source
    )


def solution(mesh):
    both = ("lon", "lat")
    in_specs = (
        P(both, None), P(both), P(None, both), P(both), P(both), P(both), P(), P(), P(),
    )
    out_specs = (P(None, both), P(both, None))
    return jax.shard_map(body, mesh=mesh, in_specs=in_specs, out_specs=out_specs, check_vma=False)
```

```python
import functools
import jax
import jax.numpy as jnp
from jax import lax
from jax.sharding import PartitionSpec as P
from jax.experimental import pallas as pl
from jax.experimental.pallas import tpu as pltpu

LEV = 64
NF = 64
G = 112
LANES = 128
SUB = 8
GB = G // SUB
PAIRS = LEV // 2
KINDS = 2
LOG2E = 1.4426950408889634
NT = (((1,), (1,)), ((), ()))
NN = (((1,), (0,)), ((), ()))


def recip(x):
    return pl.reciprocal(x, approx=True)


def mxu(a, b, dims):
    return lax.dot_general(a, b, dims, preferred_element_type=jnp.float32)


def column_kernel(
    feat_hbm, cosine_hbm, albedo_hbm, sunlit_hbm, map_hbm, gas_hbm, asym_hbm, solar_hbm, swap_hbm,
    out_hbm, mean_ref,
    feat_ref, cosine_ref, albedo_ref, sunlit_ref, map_ref, gas_ref, asym_ref, solar_ref, swap_ref,
    weight_ref, const_ref, solar_rows_ref, depth_0, depth_1, depth_2, depth_3, depth_4, depth_5, depth_6, depth_7,
    state_ref, gain_ref, add_ref, admit_ref, down_ref, net_ref,
    wide_ref, result_ref, own_ref, mask_ref, part_ref, other_ref, strip_ref, last_ref,
    small_sem, feat_sem, out_sem, send_a, recv_a, send_b, recv_b, send_c, recv_c,
):
    f32 = jnp.float32
    bf16 = jnp.bfloat16
    chunks = [
        pltpu.make_async_copy(
            feat_hbm.at[pl.ds(n * LANES, LANES), :], feat_ref.at[pl.ds(n * LANES, LANES), :], feat_sem.at[n]
        )
        for n in range(2)
    ]
    small = [
        pltpu.make_async_copy(src, dst, small_sem.at[n])
        for n, (src, dst) in enumerate(
            (
                (sunlit_hbm, sunlit_ref), (map_hbm, map_ref), (cosine_hbm, cosine_ref),
                (albedo_hbm, albedo_ref), (gas_hbm, gas_ref), (asym_hbm, asym_ref), (solar_hbm, solar_ref),
                (swap_hbm, swap_ref),
            )
        )
    ]
    for copy in chunks:
        copy.start()
    for copy in small:
        copy.start()

    n_lon, n_lat = lax.axis_size("lon"), lax.axis_size("lat")
    lon, lat = lax.axis_index("lon"), lax.axis_index("lat")
    groups = n_lon * n_lat
    chips = groups // 2
    core = lax.rem(lon, 2)
    chip = lax.div(lon, 2) * n_lat + lat
    mesh_ids = pl.DeviceIdType.MESH
    sibling = (lon + 1 - 2 * core, lat)
    peers = [
        (lax.rem(lon + 2 * a, n_lon), lax.rem(lat + c, n_lat))
        for a in range(n_lon // 2) for c in range(n_lat) if a or c
    ]
    barrier = pltpu.get_barrier_semaphore()
    for device in [sibling] + peers:
        pl.semaphore_signal(barrier, inc=1, device_id=device, device_id_type=mesh_ids)

    def remote(src, dst, sends, recvs, n, device):
        return pltpu.make_async_remote_copy(
            src_ref=src, dst_ref=dst, send_sem=sends.at[n], recv_sem=recvs.at[n],
            device_id=device, device_id_type=mesh_ids,
        )

    mask_copies = [
        remote(own_ref.at[0], mask_ref.at[core, chip], send_a, recv_a, n, device)
        for n, device in enumerate(peers)
    ]
    mask_pair = remote(mask_ref.at[core], mask_ref.at[core], send_b, recv_b, 0, sibling)

    for copy in small:
        copy.wait()

    listed = jnp.broadcast_to(swap_ref[...].astype(f32), (LANES, LANES // 2)).T
    lane_no = lax.broadcasted_iota(jnp.int32, (LANES // 2, LANES), 1).astype(f32)
    own_ref[0] = jnp.max(jnp.where(listed == lane_no, 1.0, 0.0), axis=0, keepdims=True)

    wide_ref[...] = jnp.reshape(cosine_ref[...].astype(f32), (1, 2 * LANES))
    table = gas_ref[...]
    stacked = jnp.concatenate([table, table], axis=0)
    row = lax.broadcasted_iota(jnp.int32, (2 * G, 2 * G), 0)
    col = lax.broadcasted_iota(jnp.int32, (2 * G, 2 * G), 1)
    turned = mxu(jnp.where(row == col, 1.0, 0.0).astype(bf16), stacked, NT)

    def to_rows(line):
        return jnp.broadcast_to(line, (LANES, G)).T

    asym = to_rows(asym_ref[...])
    solar_rows_ref[...] = to_rows(solar_ref[...])
    absorb = turned[:G]
    scatter = turned[G:]
    first = lax.broadcasted_iota(jnp.int32, (G, LANES), 1) < NF
    weight_ref[:G, :] = jnp.where(first, 2.0 * absorb, 2.0 * scatter).astype(bf16)
    weight_ref[G:, :] = jnp.where(first, 0.0, 2.0 * scatter).astype(bf16)
    const_ref[0] = 0.245 * (1.0 + 3.0 * asym)
    const_ref[1] = 0.98 * (0.5 - 0.25 * asym)
    const_ref[2] = 0.98 * (0.5 + 0.25 * asym)

    low_lanes = lax.broadcasted_iota(jnp.int32, (LANES, LANES), 1) < NF

    def one_block(block, carry):
        @pl.when(block == 0)
        def _():
            chunks[0].wait()

        @pl.when(block == 1)
        def _():
            chunks[1].wait()
            pl.semaphore_wait(barrier, chips)
            mask_ref[core, chip] = own_ref[0]
            for copy in mask_copies:
                copy.start()

        lanes = pl.ds(pl.multiple_of(block * LANES, LANES), LANES)
        cosine = wide_ref[:, lanes]
        slant = jnp.broadcast_to((-0.5 * LOG2E) / cosine, (SUB, LANES))
        alb_dir = jnp.broadcast_to(albedo_ref[0:1, lanes].astype(f32), (SUB, LANES))
        alb_dif = jnp.broadcast_to(albedo_ref[1:2, lanes].astype(f32), (SUB, LANES))
        state_ref[0] = solar_rows_ref[...] * (cosine * sunlit_ref[:, lanes].astype(f32))
        state_ref[1] = jnp.ones((G, LANES), f32)
        state_ref[2] = jnp.zeros((G, LANES), f32)
        state_ref[3] = jnp.zeros((G, LANES), f32)

        def optical(pair, depth, guard=None):
            chunk = feat_ref[lanes, pl.ds(pl.multiple_of(pair * LANES, LANES), LANES)]
            if guard is not None:
                chunk = chunk + guard
            turn = chunk.T
            both = jnp.concatenate(
                [
                    jnp.concatenate([turn[:NF], turn[:NF]], axis=0),
                    jnp.concatenate([turn[NF:], turn[NF:]], axis=0),
                ],
                axis=1,
            )
            depth[...] = mxu(weight_ref[...], both, NN)

        def one_pair(pair, depth):
            totals = [jnp.zeros((SUB, LANES), f32) for _ in range(2)]
            for g in range(GB):
                rows = pl.ds(g * SUB, SUB)
                direct, admit, source, left = (state_ref[n, rows, :] for n in range(4))
                slope, to_up, to_dn = (const_ref[n, rows, :] for n in range(3))
                for odd in range(2):
                    layer = 2 * pair + odd
                    tau, ray = (
                        depth[n * G + g * SUB : n * G + (g + 1) * SUB, odd * LANES : (odd + 1) * LANES]
                        for n in range(KINDS)
                    )
                    t_one = tau - 0.98 * ray
                    t_two = tau - slope * ray
                    product = t_one * t_two
                    root = lax.rsqrt(product)
                    x = product * root
                    sigma = t_one * root
                    th = jnp.tanh(x)
                    e = jnp.exp2(x * (-LOG2E))
                    sech = e + e * th
                    below = direct * jnp.exp2(tau * slant)
                    lost = (direct - below) * recip(tau) * ray
                    up = to_up * lost
                    dn = to_dn * lost
                    jump = up - left
                    totals[odd] = totals[odd] + (source + direct)
                    inner = source + up - admit * jump
                    z = recip(sigma + admit * th)
                    zs = z * sigma
                    gain = sech * zs
                    gain_ref[layer, rows, :] = gain
                    add_ref[layer, rows, :] = (th * z) * inner + jump
                    admit_ref[layer, rows, :] = admit
                    admit = (admit + sigma * th) * zs
                    source = gain * inner + dn
                    direct = below
                    left = dn
                for n, value in enumerate((direct, admit, source, left)):
                    state_ref[n, rows, :] = value
            for odd in range(2):
                down_ref[2 * pair + odd] = totals[odd]
            return jnp.minimum(th[0:1], 0.0).astype(bf16)

        optical(0, depth_0)
        optical(1, depth_1)
        optical(2, depth_2)
        optical(3, depth_3)

        def down(step, inner_carry):
            guard = None
            next_guard = one_pair(8 * step + 0, depth_0)
            optical(8 * step + 4, depth_4, guard)
            guard = next_guard
            next_guard = one_pair(8 * step + 1, depth_1)
            optical(8 * step + 5, depth_5, guard)
            guard = next_guard
            next_guard = one_pair(8 * step + 2, depth_2)
            optical(8 * step + 6, depth_6, guard)
            guard = next_guard
            next_guard = one_pair(8 * step + 3, depth_3)
            optical(8 * step + 7, depth_7, guard)
            guard = next_guard
            next_guard = one_pair(8 * step + 4, depth_4)
            optical(jnp.minimum(8 * step + 8, PAIRS - 1), depth_0, guard)
            guard = next_guard
            next_guard = one_pair(8 * step + 5, depth_5)
            optical(jnp.minimum(8 * step + 9, PAIRS - 1), depth_1, guard)
            guard = next_guard
            next_guard = one_pair(8 * step + 6, depth_6)
            optical(jnp.minimum(8 * step + 10, PAIRS - 1), depth_2, guard)
            guard = next_guard
            next_guard = one_pair(8 * step + 7, depth_7)
            optical(jnp.minimum(8 * step + 11, PAIRS - 1), depth_3, guard)
            guard = next_guard
            return inner_carry

        lax.fori_loop(0, PAIRS // 8, down, 0)

        @pl.when(block == 1)
        def _():
            for copy in mask_copies:
                copy.wait()
            mask_pair.start()

        fluxes = []
        total = jnp.zeros((SUB, LANES), f32)
        for g in range(GB):
            rows = pl.ds(g * SUB, SUB)
            direct, admit, source, left = (state_ref[n, rows, :] for n in range(4))
            over = source * (1.0 + alb_dif) + 2.0 * alb_dir * direct - left * (1.0 - alb_dif)
            flux = over / ((1.0 - alb_dif) + admit * (1.0 + alb_dif))
            total = total + (direct + source - admit * flux)
            fluxes.append(flux)
        net_ref[LEV : LEV + 1, :] = jnp.sum(total, axis=0, keepdims=True)

        def upward(step, fluxes):
            for odd in range(4):
                layer = LEV - 1 - 4 * step - odd
                total = down_ref[layer]
                out = []
                for g in range(GB):
                    rows = pl.ds(g * SUB, SUB)
                    flux = gain_ref[layer, rows, :] * fluxes[g] + add_ref[layer, rows, :]
                    total = total - admit_ref[layer, rows, :] * flux
                    out.append(flux)
                fluxes = tuple(out)
                net_ref[pl.ds(layer, 1), :] = jnp.sum(total, axis=0, keepdims=True)
            return fluxes

        lax.fori_loop(0, LEV // 4, upward, tuple(fluxes))
        live = map_ref[:, lanes] >= 0
        result_ref[:, lanes] = jnp.where(live, net_ref[0:LEV, :] - net_ref[1 : LEV + 1, :], 0.0)
        return carry

    lax.fori_loop(0, 2, one_block, 0)
    out_copy = pltpu.make_async_copy(result_ref, out_hbm, out_sem.at[0])
    out_copy.start()
    mask_pair.wait()

    place = map_ref[...]
    home = lax.shift_right_arithmetic(place, 7)
    home_core = lax.rem(lax.div(home, n_lat), 2)
    home_chip = lax.div(home, 2 * n_lat) * n_lat + lax.rem(home, n_lat)
    away_chip = jnp.where(home_chip >= chips // 2, home_chip - chips // 2, home_chip + chips // 2)
    slot = place & (LANES - 1)
    slots = place.shape[1]
    group_row = lax.broadcasted_iota(jnp.int32, (groups, slots), 0)
    at_home = jnp.where(home_core * chips + home_chip == group_row, 1.0, 0.0).astype(bf16)
    at_slot = jnp.where(slot == lax.broadcasted_iota(jnp.int32, (LANES, slots), 0), 1.0, 0.0)
    masks = mask_ref[...].reshape(groups, LANES)
    listed_at = mxu(masks.T.astype(bf16), at_home, NN)
    moved = jnp.sum(listed_at * at_slot, axis=0, keepdims=True)
    held = home_core * chips + jnp.where(moved > 0.5, away_chip, home_chip)
    held = jnp.where(place < 0, -1, held)
    member = jnp.where(held == group_row, 1.0, 0.0).astype(bf16)
    absorbed = jnp.concatenate([result_ref[...], jnp.zeros((LANES - LEV, slots), f32)], axis=0)
    high = absorbed.astype(bf16)
    low = (absorbed - high.astype(f32)).astype(bf16)
    part_ref[...] = (mxu(member, high, NT) + mxu(member, low, NT)).reshape(2, chips, LANES)

    copy = remote(part_ref.at[1 - core], other_ref, send_b, recv_b, 1, sibling)
    copy.start()
    copy.wait()
    strip_ref[...] = (part_ref[core] + other_ref[...]).reshape(chips, 1, LANES)
    copies = [
        remote(strip_ref.at[lax.div(device[0], 2) * n_lat + device[1]], last_ref.at[n], send_c, recv_c, n, device)
        for n, device in enumerate(peers)
    ]
    for copy in copies:
        copy.start()
    for copy in copies:
        copy.wait()
    total = strip_ref[chip] + jnp.sum(last_ref[...], axis=0)
    mean_ref[...] = total[:, :LEV] * (1.0 / LANES)
    out_copy.wait()


def columns_absorbed(features, cosine, albedo, sunlit, column_map, swap_list, gas_table, asymmetry, solar):
    anywhere = pl.BlockSpec(memory_space=pl.ANY)
    vmem = pl.BlockSpec(memory_space=pltpu.VMEM)
    f32, bf16, i32 = jnp.float32, jnp.bfloat16, jnp.int32
    chips = lax.axis_size("lon") * lax.axis_size("lat") // 2
    dma = pltpu.SemaphoreType.DMA
    return pl.pallas_call(
        column_kernel,
        out_shape=(jax.ShapeDtypeStruct((LEV, 2 * LANES), f32), jax.ShapeDtypeStruct((1, LEV), f32)),
        in_specs=[anywhere] * 9,
        out_specs=(anywhere, vmem),
        scratch_shapes=[
            pltpu.VMEM((2 * LANES, LEV * NF), bf16),
            pltpu.VMEM((2 * LANES,), bf16),
            pltpu.VMEM((2, 2 * LANES), bf16),
            pltpu.VMEM((1, 2 * LANES), i32),
            pltpu.VMEM((1, 2 * LANES), i32),
            pltpu.VMEM((NF, 2 * G), bf16),
            pltpu.VMEM((1, G), f32),
            pltpu.VMEM((1, G), f32),
            pltpu.VMEM((1, LANES // 2), i32),
            pltpu.VMEM((KINDS * G, LANES), bf16),
            pltpu.VMEM((3, G, LANES), f32),
            pltpu.VMEM((G, LANES), f32),
            pltpu.VMEM((KINDS * G, 2 * LANES), f32),
            pltpu.VMEM((KINDS * G, 2 * LANES), f32),
            pltpu.VMEM((KINDS * G, 2 * LANES), f32),
            pltpu.VMEM((KINDS * G, 2 * LANES), f32),
            pltpu.VMEM((KINDS * G, 2 * LANES), f32),
            pltpu.VMEM((KINDS * G, 2 * LANES), f32),
            pltpu.VMEM((KINDS * G, 2 * LANES), f32),
            pltpu.VMEM((KINDS * G, 2 * LANES), f32),
            pltpu.VMEM((4, G, LANES), f32),
            pltpu.VMEM((LEV, G, LANES), f32),
            pltpu.VMEM((LEV, G, LANES), f32),
            pltpu.VMEM((LEV, G, LANES), f32),
            pltpu.VMEM((LEV, SUB, LANES), f32),
            pltpu.VMEM((LEV + SUB, LANES), f32),
            pltpu.VMEM((1, 2 * LANES), f32),
            pltpu.VMEM((LEV, 2 * LANES), f32),
            pltpu.VMEM((1, 1, LANES), f32),
            pltpu.VMEM((2, chips, 1, LANES), f32),
            pltpu.VMEM((2, chips, LANES), f32),
            pltpu.VMEM((chips, LANES), f32),
            pltpu.VMEM((chips, 1, LANES), f32),
            pltpu.VMEM((chips - 1, 1, LANES), f32),
            dma((8,)), dma((2,)), dma((2,)), dma((chips,)), dma((chips,)), dma((2,)), dma((2,)), dma((chips,)), dma((chips,)),
        ],
        compiler_params=pltpu.CompilerParams(collective_id=0, has_side_effects=True, vmem_limit_bytes=60 * 1024 * 1024),
        cost_estimate=pl.CostEstimate(flops=200_000_000, bytes_accessed=2_200_000, transcendentals=10_000_000),
    )(features, cosine, albedo, sunlit[None], column_map[None], gas_table, asymmetry[None], solar[None], swap_list[None])


def finish_kernel(absorbed_hbm, mean_hbm, absorbed_out, mean_out, sems):
    copies = [
        pltpu.make_async_copy(absorbed_hbm, absorbed_out, sems.at[0]),
        pltpu.make_async_copy(mean_hbm, mean_out, sems.at[1]),
    ]
    for copy in copies:
        copy.start()
    for copy in copies:
        copy.wait()


def finished(absorbed, mean):
    anywhere = pl.BlockSpec(memory_space=pl.ANY)
    return pl.pallas_call(
        finish_kernel,
        out_shape=(
            jax.ShapeDtypeStruct(absorbed.shape, absorbed.dtype), jax.ShapeDtypeStruct(mean.shape, mean.dtype)
        ),
        in_specs=[anywhere] * 2,
        out_specs=(anywhere, anywhere),
        scratch_shapes=[pltpu.SemaphoreType.DMA((2,))],
        compiler_params=pltpu.CompilerParams(vmem_limit_bytes=60 * 1024 * 1024),
    )(absorbed, mean)


def body(
    features, cosine_zenith, albedo, sunlit, column_map, swap_list, gas_table, asymmetry, solar_source
):
    absorbed, mean = columns_absorbed(
        features, cosine_zenith, albedo, sunlit, column_map, swap_list, gas_table, asymmetry, solar_source
    )
    return finished(absorbed, mean)


def solution(mesh):
    both = ("lon", "lat")
    in_specs = (
        P(both, None), P(both), P(None, both), P(both), P(both), P(both), P(), P(), P(),
    )
    out_specs = (P(None, both), P(both, None))
    return jax.shard_map(body, mesh=mesh, in_specs=in_specs, out_specs=out_specs, check_vma=False)
```

```python
import functools
import jax
import jax.numpy as jnp
from jax import lax
from jax.sharding import PartitionSpec as P
from jax.experimental import pallas as pl
from jax.experimental.pallas import tpu as pltpu

LEV = 64
NF = 64
G = 112
LANES = 128
SUB = 8
GB = G // SUB
PAIRS = LEV // 2
KINDS = 2
LOG2E = 1.4426950408889634
NT = (((1,), (1,)), ((), ()))
NN = (((1,), (0,)), ((), ()))


def recip(x):
    return pl.reciprocal(x, approx=True)


def mxu(a, b, dims):
    return lax.dot_general(a, b, dims, preferred_element_type=jnp.float32)


def column_kernel(
    feat_hbm, cosine_hbm, albedo_hbm, sunlit_hbm, map_hbm, gas_hbm, asym_hbm, solar_hbm, swap_hbm,
    out_hbm, sum_ref,
    feat_ref, cosine_ref, albedo_ref, sunlit_ref, map_ref, gas_ref, asym_ref, solar_ref, swap_ref,
    weight_ref, const_ref, solar_rows_ref, depth_0, depth_1, depth_2, depth_3, depth_4, depth_5, depth_6, depth_7,
    state_ref, gain_ref, add_ref, admit_ref, down_ref, net_ref,
    wide_ref, result_ref, own_ref, mask_ref, part_ref, other_ref, strip_ref, last_ref,
    small_sem, feat_sem, out_sem, send_a, recv_a, send_b, recv_b, send_c, recv_c,
):
    f32 = jnp.float32
    bf16 = jnp.bfloat16
    chunks = [
        pltpu.make_async_copy(
            feat_hbm.at[pl.ds(n * LANES, LANES), :], feat_ref.at[pl.ds(n * LANES, LANES), :], feat_sem.at[n]
        )
        for n in range(2)
    ]
    small = [
        pltpu.make_async_copy(src, dst, small_sem.at[n])
        for n, (src, dst) in enumerate(
            (
                (sunlit_hbm, sunlit_ref), (map_hbm, map_ref), (cosine_hbm, cosine_ref),
                (albedo_hbm, albedo_ref), (gas_hbm, gas_ref), (asym_hbm, asym_ref), (solar_hbm, solar_ref),
                (swap_hbm, swap_ref),
            )
        )
    ]
    for copy in chunks:
        copy.start()
    for copy in small:
        copy.start()

    n_lon, n_lat = lax.axis_size("lon"), lax.axis_size("lat")
    lon, lat = lax.axis_index("lon"), lax.axis_index("lat")
    groups = n_lon * n_lat
    chips = groups // 2
    core = lax.rem(lon, 2)
    chip = lax.div(lon, 2) * n_lat + lat
    mesh_ids = pl.DeviceIdType.MESH
    sibling = (lon + 1 - 2 * core, lat)
    peers = [
        (lax.rem(lon + 2 * a, n_lon), lax.rem(lat + c, n_lat))
        for a in range(n_lon // 2) for c in range(n_lat) if a or c
    ]
    barrier = pltpu.get_barrier_semaphore()
    for device in [sibling] + peers:
        pl.semaphore_signal(barrier, inc=1, device_id=device, device_id_type=mesh_ids)

    def remote(src, dst, sends, recvs, n, device):
        return pltpu.make_async_remote_copy(
            src_ref=src, dst_ref=dst, send_sem=sends.at[n], recv_sem=recvs.at[n],
            device_id=device, device_id_type=mesh_ids,
        )

    mask_copies = [
        remote(own_ref.at[0], mask_ref.at[core, chip], send_a, recv_a, n, device)
        for n, device in enumerate(peers)
    ]
    mask_pair = remote(mask_ref.at[core], mask_ref.at[core], send_b, recv_b, 0, sibling)

    for copy in small:
        copy.wait()

    listed = jnp.broadcast_to(swap_ref[...].astype(f32), (LANES, LANES // 2)).T
    lane_no = lax.broadcasted_iota(jnp.int32, (LANES // 2, LANES), 1).astype(f32)
    own_ref[0] = jnp.max(jnp.where(listed == lane_no, 1.0, 0.0), axis=0, keepdims=True)

    wide_ref[...] = jnp.reshape(cosine_ref[...].astype(f32), (1, 2 * LANES))
    table = gas_ref[...]
    stacked = jnp.concatenate([table, table], axis=0)
    row = lax.broadcasted_iota(jnp.int32, (2 * G, 2 * G), 0)
    col = lax.broadcasted_iota(jnp.int32, (2 * G, 2 * G), 1)
    turned = mxu(jnp.where(row == col, 1.0, 0.0).astype(bf16), stacked, NT)

    def to_rows(line):
        return jnp.broadcast_to(line, (LANES, G)).T

    asym = to_rows(asym_ref[...])
    solar_rows_ref[...] = to_rows(solar_ref[...])
    absorb = turned[:G]
    scatter = turned[G:]
    first = lax.broadcasted_iota(jnp.int32, (G, LANES), 1) < NF
    weight_ref[:G, :] = jnp.where(first, 2.0 * absorb, 2.0 * scatter).astype(bf16)
    weight_ref[G:, :] = jnp.where(first, 0.0, 2.0 * scatter).astype(bf16)
    const_ref[0] = 0.245 * (1.0 + 3.0 * asym)
    const_ref[1] = 0.98 * (0.5 - 0.25 * asym)
    const_ref[2] = 0.98 * (0.5 + 0.25 * asym)

    low_lanes = lax.broadcasted_iota(jnp.int32, (LANES, LANES), 1) < NF

    def one_block(block, carry):
        @pl.when(block == 0)
        def _():
            chunks[0].wait()

        @pl.when(block == 1)
        def _():
            chunks[1].wait()
            pl.semaphore_wait(barrier, chips)
            mask_ref[core, chip] = own_ref[0]
            for copy in mask_copies:
                copy.start()

        lanes = pl.ds(pl.multiple_of(block * LANES, LANES), LANES)
        cosine = wide_ref[:, lanes]
        slant = jnp.broadcast_to((-0.5 * LOG2E) / cosine, (SUB, LANES))
        alb_dir = jnp.broadcast_to(albedo_ref[0:1, lanes].astype(f32), (SUB, LANES))
        alb_dif = jnp.broadcast_to(albedo_ref[1:2, lanes].astype(f32), (SUB, LANES))
        state_ref[0] = solar_rows_ref[...] * (cosine * sunlit_ref[:, lanes].astype(f32))
        state_ref[1] = jnp.ones((G, LANES), f32)
        state_ref[2] = jnp.zeros((G, LANES), f32)
        state_ref[3] = jnp.zeros((G, LANES), f32)

        def optical(pair, depth, guard=None):
            chunk = feat_ref[lanes, pl.ds(pl.multiple_of(pair * LANES, LANES), LANES)]
            if guard is not None:
                chunk = chunk + guard
            turn = chunk.T
            both = jnp.concatenate(
                [
                    jnp.concatenate([turn[:NF], turn[:NF]], axis=0),
                    jnp.concatenate([turn[NF:], turn[NF:]], axis=0),
                ],
                axis=1,
            )
            depth[...] = mxu(weight_ref[...], both, NN)

        def one_pair(pair, depth):
            totals = [jnp.zeros((SUB, LANES), f32) for _ in range(2)]
            for g in range(GB):
                rows = pl.ds(g * SUB, SUB)
                direct, admit, source, left = (state_ref[n, rows, :] for n in range(4))
                slope, to_up, to_dn = (const_ref[n, rows, :] for n in range(3))
                for odd in range(2):
                    layer = 2 * pair + odd
                    tau, ray = (
                        depth[n * G + g * SUB : n * G + (g + 1) * SUB, odd * LANES : (odd + 1) * LANES]
                        for n in range(KINDS)
                    )
                    t_one = tau - 0.98 * ray
                    t_two = tau - slope * ray
                    product = t_one * t_two
                    root = lax.rsqrt(product)
                    x = product * root
                    sigma = t_one * root
                    th = jnp.tanh(x)
                    e = jnp.exp2(x * (-LOG2E))
                    sech = e + e * th
                    below = direct * jnp.exp2(tau * slant)
                    lost = (direct - below) * recip(tau) * ray
                    up = to_up * lost
                    dn = to_dn * lost
                    jump = up - left
                    totals[odd] = totals[odd] + (source + direct)
                    inner = source + up - admit * jump
                    z = recip(sigma + admit * th)
                    zs = z * sigma
                    gain = sech * zs
                    gain_ref[layer, rows, :] = gain
                    add_ref[layer, rows, :] = (th * z) * inner + jump
                    admit_ref[layer, rows, :] = admit
                    admit = (admit + sigma * th) * zs
                    source = gain * inner + dn
                    direct = below
                    left = dn
                for n, value in enumerate((direct, admit, source, left)):
                    state_ref[n, rows, :] = value
            for odd in range(2):
                down_ref[2 * pair + odd] = totals[odd]
            return jnp.minimum(th[0:1], 0.0).astype(bf16)

        optical(0, depth_0)
        optical(1, depth_1)
        optical(2, depth_2)
        optical(3, depth_3)

        def down(step, inner_carry):
            guard = None
            next_guard = one_pair(8 * step + 0, depth_0)
            optical(8 * step + 4, depth_4, guard)
            guard = next_guard
            next_guard = one_pair(8 * step + 1, depth_1)
            optical(8 * step + 5, depth_5, guard)
            guard = next_guard
            next_guard = one_pair(8 * step + 2, depth_2)
            optical(8 * step + 6, depth_6, guard)
            guard = next_guard
            next_guard = one_pair(8 * step + 3, depth_3)
            optical(8 * step + 7, depth_7, guard)
            guard = next_guard
            next_guard = one_pair(8 * step + 4, depth_4)
            optical(jnp.minimum(8 * step + 8, PAIRS - 1), depth_0, guard)
            guard = next_guard
            next_guard = one_pair(8 * step + 5, depth_5)
            optical(jnp.minimum(8 * step + 9, PAIRS - 1), depth_1, guard)
            guard = next_guard
            next_guard = one_pair(8 * step + 6, depth_6)
            optical(jnp.minimum(8 * step + 10, PAIRS - 1), depth_2, guard)
            guard = next_guard
            next_guard = one_pair(8 * step + 7, depth_7)
            optical(jnp.minimum(8 * step + 11, PAIRS - 1), depth_3, guard)
            guard = next_guard
            return inner_carry

        lax.fori_loop(0, PAIRS // 8, down, 0)

        @pl.when(block == 1)
        def _():
            for copy in mask_copies:
                copy.wait()
            mask_pair.start()

        fluxes = []
        total = jnp.zeros((SUB, LANES), f32)
        for g in range(GB):
            rows = pl.ds(g * SUB, SUB)
            direct, admit, source, left = (state_ref[n, rows, :] for n in range(4))
            over = source * (1.0 + alb_dif) + 2.0 * alb_dir * direct - left * (1.0 - alb_dif)
            flux = over / ((1.0 - alb_dif) + admit * (1.0 + alb_dif))
            total = total + (direct + source - admit * flux)
            fluxes.append(flux)
        net_ref[LEV : LEV + 1, :] = jnp.sum(total, axis=0, keepdims=True)

        def upward(step, fluxes):
            for odd in range(4):
                layer = LEV - 1 - 4 * step - odd
                total = down_ref[layer]
                out = []
                for g in range(GB):
                    rows = pl.ds(g * SUB, SUB)
                    flux = gain_ref[layer, rows, :] * fluxes[g] + add_ref[layer, rows, :]
                    total = total - admit_ref[layer, rows, :] * flux
                    out.append(flux)
                fluxes = tuple(out)
                net_ref[pl.ds(layer, 1), :] = jnp.sum(total, axis=0, keepdims=True)
            return fluxes

        lax.fori_loop(0, LEV // 4, upward, tuple(fluxes))
        result_ref[:, lanes] = net_ref[0:LEV, :] - net_ref[1 : LEV + 1, :]
        return carry

    lax.fori_loop(0, 2, one_block, 0)
    out_copy = pltpu.make_async_copy(result_ref, out_hbm, out_sem.at[0])
    out_copy.start()
    mask_pair.wait()

    place = map_ref[...]
    home = lax.shift_right_arithmetic(place, 7)
    home_core = lax.rem(lax.div(home, n_lat), 2)
    home_chip = lax.div(home, 2 * n_lat) * n_lat + lax.rem(home, n_lat)
    away_chip = jnp.where(home_chip >= chips // 2, home_chip - chips // 2, home_chip + chips // 2)
    slot = place & (LANES - 1)
    slots = place.shape[1]
    group_row = lax.broadcasted_iota(jnp.int32, (groups, slots), 0)
    at_home = jnp.where(home_core * chips + home_chip == group_row, 1.0, 0.0).astype(bf16)
    at_slot = jnp.where(slot == lax.broadcasted_iota(jnp.int32, (LANES, slots), 0), 1.0, 0.0)
    masks = mask_ref[...].reshape(groups, LANES)
    listed_at = mxu(masks.T.astype(bf16), at_home, NN)
    moved = jnp.sum(listed_at * at_slot, axis=0, keepdims=True)
    held = home_core * chips + jnp.where(moved > 0.5, away_chip, home_chip)
    held = jnp.where(place < 0, -1, held)
    member = jnp.where(held == group_row, 1.0, 0.0).astype(bf16)
    absorbed = jnp.where(place < 0, 0.0, result_ref[...])
    absorbed = jnp.concatenate([absorbed, jnp.zeros((LANES - LEV, slots), f32)], axis=0)
    high = absorbed.astype(bf16)
    low = (absorbed - high.astype(f32)).astype(bf16)
    part_ref[...] = (mxu(member, high, NT) + mxu(member, low, NT)).reshape(2, chips, LANES)

    copy = remote(part_ref.at[1 - core], other_ref, send_b, recv_b, 1, sibling)
    copy.start()
    copy.wait()
    strip_ref[...] = (part_ref[core] + other_ref[...]).reshape(chips, 1, LANES)
    copies = [
        remote(strip_ref.at[lax.div(device[0], 2) * n_lat + device[1]], last_ref.at[n], send_c, recv_c, n, device)
        for n, device in enumerate(peers)
    ]
    for copy in copies:
        copy.start()
    for copy in copies:
        copy.wait()
    total = strip_ref[chip] + jnp.sum(last_ref[...], axis=0)
    sum_ref[...] = total[:, :LEV]
    out_copy.wait()


def columns_absorbed(features, cosine, albedo, sunlit, column_map, swap_list, gas_table, asymmetry, solar):
    anywhere = pl.BlockSpec(memory_space=pl.ANY)
    vmem = pl.BlockSpec(memory_space=pltpu.VMEM)
    f32, bf16, i32 = jnp.float32, jnp.bfloat16, jnp.int32
    chips = lax.axis_size("lon") * lax.axis_size("lat") // 2
    dma = pltpu.SemaphoreType.DMA
    return pl.pallas_call(
        column_kernel,
        out_shape=(jax.ShapeDtypeStruct((LEV, 2 * LANES), f32), jax.ShapeDtypeStruct((1, LEV), f32)),
        in_specs=[anywhere] * 9,
        out_specs=(anywhere, vmem),
        scratch_shapes=[
            pltpu.VMEM((2 * LANES, LEV * NF), bf16),
            pltpu.VMEM((2 * LANES,), bf16),
            pltpu.VMEM((2, 2 * LANES), bf16),
            pltpu.VMEM((1, 2 * LANES), i32),
            pltpu.VMEM((1, 2 * LANES), i32),
            pltpu.VMEM((NF, 2 * G), bf16),
            pltpu.VMEM((1, G), f32),
            pltpu.VMEM((1, G), f32),
            pltpu.VMEM((1, LANES // 2), i32),
            pltpu.VMEM((KINDS * G, LANES), bf16),
            pltpu.VMEM((3, G, LANES), f32),
            pltpu.VMEM((G, LANES), f32),
            pltpu.VMEM((KINDS * G, 2 * LANES), f32),
            pltpu.VMEM((KINDS * G, 2 * LANES), f32),
            pltpu.VMEM((KINDS * G, 2 * LANES), f32),
            pltpu.VMEM((KINDS * G, 2 * LANES), f32),
            pltpu.VMEM((KINDS * G, 2 * LANES), f32),
            pltpu.VMEM((KINDS * G, 2 * LANES), f32),
            pltpu.VMEM((KINDS * G, 2 * LANES), f32),
            pltpu.VMEM((KINDS * G, 2 * LANES), f32),
            pltpu.VMEM((4, G, LANES), f32),
            pltpu.VMEM((LEV, G, LANES), f32),
            pltpu.VMEM((LEV, G, LANES), f32),
            pltpu.VMEM((LEV, G, LANES), f32),
            pltpu.VMEM((LEV, SUB, LANES), f32),
            pltpu.VMEM((LEV + SUB, LANES), f32),
            pltpu.VMEM((1, 2 * LANES), f32),
            pltpu.VMEM((LEV, 2 * LANES), f32),
            pltpu.VMEM((1, 1, LANES), f32),
            pltpu.VMEM((2, chips, 1, LANES), f32),
            pltpu.VMEM((2, chips, LANES), f32),
            pltpu.VMEM((chips, LANES), f32),
            pltpu.VMEM((chips, 1, LANES), f32),
            pltpu.VMEM((chips - 1, 1, LANES), f32),
            dma((8,)), dma((2,)), dma((2,)), dma((chips,)), dma((chips,)), dma((2,)), dma((2,)), dma((chips,)), dma((chips,)),
        ],
        compiler_params=pltpu.CompilerParams(collective_id=0, has_side_effects=True, vmem_limit_bytes=60 * 1024 * 1024),
        cost_estimate=pl.CostEstimate(flops=200_000_000, bytes_accessed=2_200_000, transcendentals=10_000_000),
    )(features, cosine, albedo, sunlit[None], column_map[None], gas_table, asymmetry[None], solar[None], swap_list[None])

def body(
    features, cosine_zenith, albedo, sunlit, column_map, swap_list, gas_table, asymmetry, solar_source
):
    absorbed, sums = columns_absorbed(
        features, cosine_zenith, albedo, sunlit, column_map, swap_list, gas_table, asymmetry, solar_source
    )
    live = column_map[None] >= 0
    return jnp.where(live, absorbed, 0.0), sums * (1.0 / LANES)


def solution(mesh):
    both = ("lon", "lat")
    in_specs = (
        P(both, None), P(both), P(None, both), P(both), P(both), P(both), P(), P(), P(),
    )
    out_specs = (P(None, both), P(both, None))
    return jax.shard_map(body, mesh=mesh, in_specs=in_specs, out_specs=out_specs, check_vma=False)
```

```python
import functools
import jax
import jax.numpy as jnp
from jax import lax
from jax.sharding import PartitionSpec as P
from jax.experimental import pallas as pl
from jax.experimental.pallas import tpu as pltpu

LEV = 64
NF = 64
G = 112
LANES = 128
SUB = 8
GB = G // SUB
PAIRS = LEV // 2
KINDS = 2
LOG2E = 1.4426950408889634
NT = (((1,), (1,)), ((), ()))
NN = (((1,), (0,)), ((), ()))


def recip(x):
    return pl.reciprocal(x, approx=True)


def mxu(a, b, dims):
    return lax.dot_general(a, b, dims, preferred_element_type=jnp.float32)


def column_kernel(
    feat_hbm, cosine_hbm, albedo_hbm, sunlit_hbm, map_hbm, gas_hbm, asym_hbm, solar_hbm, swap_hbm,
    out_hbm, mean_ref,
    feat_ref, cosine_ref, albedo_ref, sunlit_ref, map_ref, gas_ref, asym_ref, solar_ref, swap_ref,
    weight_ref, const_ref, solar_rows_ref, depth_0, depth_1, depth_2, depth_3, depth_4, depth_5, depth_6, depth_7,
    state_ref, gain_ref, add_ref, admit_ref, down_ref, net_ref,
    wide_ref, result_ref, member_ref, own_ref, mask_ref, part_ref, other_ref, strip_ref, last_ref,
    small_sem, feat_sem, out_sem, send_a, recv_a, send_b, recv_b, send_c, recv_c,
):
    f32 = jnp.float32
    bf16 = jnp.bfloat16
    chunks = [
        pltpu.make_async_copy(
            feat_hbm.at[pl.ds(n * LANES, LANES), :], feat_ref.at[pl.ds(n * LANES, LANES), :], feat_sem.at[n]
        )
        for n in range(2)
    ]
    small = [
        pltpu.make_async_copy(src, dst, small_sem.at[n])
        for n, (src, dst) in enumerate(
            (
                (sunlit_hbm, sunlit_ref), (map_hbm, map_ref), (cosine_hbm, cosine_ref),
                (albedo_hbm, albedo_ref), (gas_hbm, gas_ref), (asym_hbm, asym_ref), (solar_hbm, solar_ref),
                (swap_hbm, swap_ref),
            )
        )
    ]
    for copy in chunks:
        copy.start()
    for copy in small:
        copy.start()

    n_lon, n_lat = lax.axis_size("lon"), lax.axis_size("lat")
    lon, lat = lax.axis_index("lon"), lax.axis_index("lat")
    groups = n_lon * n_lat
    chips = groups // 2
    core = lax.rem(lon, 2)
    chip = lax.div(lon, 2) * n_lat + lat
    mesh_ids = pl.DeviceIdType.MESH
    sibling = (lon + 1 - 2 * core, lat)
    n_x, n_z = n_lon // 4, n_lat // 2
    steps = [
        (dx, high, dz, low_bit)
        for dx in range(n_x) for high in range(2) for dz in range(n_z) for low_bit in range(2)
        if dx or high or dz or low_bit
    ]
    steps.sort(key=lambda d: -(min(d[0], n_x - d[0]) + min(d[2], n_z - d[2]) + (1 if d[3] else 2 * d[1])))
    x, y_high = lax.div(lon, 4), lax.rem(lax.div(lon, 2), 2)
    z, y_low = lax.div(lat, 2), lax.rem(lat, 2)
    peers = [
        (
            lax.rem(x + dx, n_x) * 4 + lax.rem(y_high + high, 2) * 2 + core,
            lax.rem(z + dz, n_z) * 2 + lax.rem(y_low + low_bit, 2),
        )
        for dx, high, dz, low_bit in steps
    ]
    barrier = pltpu.get_barrier_semaphore()
    for device in [sibling] + peers:
        pl.semaphore_signal(barrier, inc=1, device_id=device, device_id_type=mesh_ids)

    def remote(src, dst, sends, recvs, n, device):
        return pltpu.make_async_remote_copy(
            src_ref=src, dst_ref=dst, send_sem=sends.at[n], recv_sem=recvs.at[n],
            device_id=device, device_id_type=mesh_ids,
        )

    mask_copies = [
        remote(own_ref.at[0], mask_ref.at[core, chip], send_a, recv_a, n, device)
        for n, device in enumerate(peers)
    ]
    mask_pair = remote(mask_ref.at[core], mask_ref.at[core], send_b, recv_b, 0, sibling)

    for copy in small:
        copy.wait()

    listed = jnp.broadcast_to(swap_ref[...].astype(f32), (LANES, LANES // 2)).T
    lane_no = lax.broadcasted_iota(jnp.int32, (LANES // 2, LANES), 1).astype(f32)
    own_ref[0] = jnp.max(jnp.where(listed == lane_no, 1.0, 0.0), axis=0, keepdims=True)

    wide_ref[...] = jnp.reshape(cosine_ref[...].astype(f32), (1, 2 * LANES))
    table = gas_ref[...]
    stacked = jnp.concatenate([table, table], axis=0)
    row = lax.broadcasted_iota(jnp.int32, (2 * G, 2 * G), 0)
    col = lax.broadcasted_iota(jnp.int32, (2 * G, 2 * G), 1)
    turned = mxu(jnp.where(row == col, 1.0, 0.0).astype(bf16), stacked, NT)

    def to_rows(line):
        return jnp.broadcast_to(line, (LANES, G)).T

    asym = to_rows(asym_ref[...])
    solar_rows_ref[...] = to_rows(solar_ref[...])
    absorb = turned[:G]
    scatter = turned[G:]
    first = lax.broadcasted_iota(jnp.int32, (G, LANES), 1) < NF
    weight_ref[:G, :] = jnp.where(first, 2.0 * absorb, 2.0 * scatter).astype(bf16)
    weight_ref[G:, :] = jnp.where(first, 0.0, 2.0 * scatter).astype(bf16)
    const_ref[0] = 0.245 * (1.0 + 3.0 * asym)
    const_ref[1] = 0.98 * (0.5 - 0.25 * asym)
    const_ref[2] = 0.98 * (0.5 + 0.25 * asym)

    low_lanes = lax.broadcasted_iota(jnp.int32, (LANES, LANES), 1) < NF

    def one_block(block, carry):
        @pl.when(block == 0)
        def _():
            chunks[0].wait()

        @pl.when(block == 1)
        def _():
            chunks[1].wait()

        lanes = pl.ds(pl.multiple_of(block * LANES, LANES), LANES)
        cosine = wide_ref[:, lanes]
        slant = jnp.broadcast_to((-0.5 * LOG2E) / cosine, (SUB, LANES))
        alb_dir = jnp.broadcast_to(albedo_ref[0:1, lanes].astype(f32), (SUB, LANES))
        alb_dif = jnp.broadcast_to(albedo_ref[1:2, lanes].astype(f32), (SUB, LANES))
        state_ref[0] = solar_rows_ref[...] * (cosine * sunlit_ref[:, lanes].astype(f32))
        state_ref[1] = jnp.ones((G, LANES), f32)
        state_ref[2] = jnp.zeros((G, LANES), f32)
        state_ref[3] = jnp.zeros((G, LANES), f32)

        def optical(pair, depth, guard=None):
            chunk = feat_ref[lanes, pl.ds(pl.multiple_of(pair * LANES, LANES), LANES)]
            if guard is not None:
                chunk = chunk + guard
            turn = chunk.T
            both = jnp.concatenate(
                [
                    jnp.concatenate([turn[:NF], turn[:NF]], axis=0),
                    jnp.concatenate([turn[NF:], turn[NF:]], axis=0),
                ],
                axis=1,
            )
            depth[...] = mxu(weight_ref[...], both, NN)

        def one_pair(pair, depth):
            totals = [jnp.zeros((SUB, LANES), f32) for _ in range(2)]
            for g in range(GB):
                rows = pl.ds(g * SUB, SUB)
                direct, admit, source, left = (state_ref[n, rows, :] for n in range(4))
                slope, to_up, to_dn = (const_ref[n, rows, :] for n in range(3))
                for odd in range(2):
                    layer = 2 * pair + odd
                    tau, ray = (
                        depth[n * G + g * SUB : n * G + (g + 1) * SUB, odd * LANES : (odd + 1) * LANES]
                        for n in range(KINDS)
                    )
                    t_one = tau - 0.98 * ray
                    t_two = tau - slope * ray
                    product = t_one * t_two
                    root = lax.rsqrt(product)
                    x = product * root
                    sigma = t_one * root
                    th = jnp.tanh(x)
                    e = jnp.exp2(x * (-LOG2E))
                    sech = e + e * th
                    below = direct * jnp.exp2(tau * slant)
                    lost = (direct - below) * recip(tau) * ray
                    up = to_up * lost
                    dn = to_dn * lost
                    jump = up - left
                    totals[odd] = totals[odd] + (source + direct)
                    inner = source + up - admit * jump
                    z = recip(sigma + admit * th)
                    zs = z * sigma
                    gain = sech * zs
                    gain_ref[layer, rows, :] = gain
                    add_ref[layer, rows, :] = (th * z) * inner + jump
                    admit_ref[layer, rows, :] = admit
                    admit = (admit + sigma * th) * zs
                    source = gain * inner + dn
                    direct = below
                    left = dn
                for n, value in enumerate((direct, admit, source, left)):
                    state_ref[n, rows, :] = value
            for odd in range(2):
                down_ref[2 * pair + odd] = totals[odd]
            return jnp.minimum(th[0:1], 0.0).astype(bf16)

        optical(0, depth_0)
        optical(1, depth_1)
        optical(2, depth_2)
        optical(3, depth_3)

        def down(step, inner_carry):
            @pl.when((block == 0) & (step == PAIRS // 8 - 1))
            def _():
                pl.semaphore_wait(barrier, chips)
                mask_ref[core, chip] = own_ref[0]
                for copy in mask_copies:
                    copy.start()

            @pl.when((block == 1) & (step == PAIRS // 8 - 1))
            def _():
                for copy in mask_copies:
                    copy.wait()
                mask_pair.start()

            guard = None
            next_guard = one_pair(8 * step + 0, depth_0)
            optical(8 * step + 4, depth_4, guard)
            guard = next_guard
            next_guard = one_pair(8 * step + 1, depth_1)
            optical(8 * step + 5, depth_5, guard)
            guard = next_guard
            next_guard = one_pair(8 * step + 2, depth_2)
            optical(8 * step + 6, depth_6, guard)
            guard = next_guard
            next_guard = one_pair(8 * step + 3, depth_3)
            optical(8 * step + 7, depth_7, guard)
            guard = next_guard
            next_guard = one_pair(8 * step + 4, depth_4)
            optical(jnp.minimum(8 * step + 8, PAIRS - 1), depth_0, guard)
            guard = next_guard
            next_guard = one_pair(8 * step + 5, depth_5)
            optical(jnp.minimum(8 * step + 9, PAIRS - 1), depth_1, guard)
            guard = next_guard
            next_guard = one_pair(8 * step + 6, depth_6)
            optical(jnp.minimum(8 * step + 10, PAIRS - 1), depth_2, guard)
            guard = next_guard
            next_guard = one_pair(8 * step + 7, depth_7)
            optical(jnp.minimum(8 * step + 11, PAIRS - 1), depth_3, guard)
            guard = next_guard
            return inner_carry

        lax.fori_loop(0, PAIRS // 8, down, 0)

        @pl.when(block == 1)
        def _():
            mask_pair.wait()

            place = map_ref[...]
            home = lax.shift_right_arithmetic(place, 7)
            home_core = lax.rem(lax.div(home, n_lat), 2)
            home_chip = lax.div(home, 2 * n_lat) * n_lat + lax.rem(home, n_lat)
            away_chip = jnp.where(home_chip >= chips // 2, home_chip - chips // 2, home_chip + chips // 2)
            slot = place & (LANES - 1)
            slots = place.shape[1]
            group_row = lax.broadcasted_iota(jnp.int32, (groups, slots), 0)
            at_home = jnp.where(home_core * chips + home_chip == group_row, 1.0, 0.0).astype(bf16)
            at_slot = jnp.where(slot == lax.broadcasted_iota(jnp.int32, (LANES, slots), 0), 1.0, 0.0)
            masks = mask_ref[...].reshape(groups, LANES)
            listed_at = mxu(masks.T.astype(bf16), at_home, NN)
            moved = jnp.sum(listed_at * at_slot, axis=0, keepdims=True)
            held = home_core * chips + jnp.where(moved > 0.5, away_chip, home_chip)
            held = jnp.where(place < 0, -1, held)
            member_ref[...] = jnp.where(held == group_row, 1.0, 0.0).astype(bf16)

        fluxes = []
        total = jnp.zeros((SUB, LANES), f32)
        for g in range(GB):
            rows = pl.ds(g * SUB, SUB)
            direct, admit, source, left = (state_ref[n, rows, :] for n in range(4))
            over = source * (1.0 + alb_dif) + 2.0 * alb_dir * direct - left * (1.0 - alb_dif)
            flux = over / ((1.0 - alb_dif) + admit * (1.0 + alb_dif))
            total = total + (direct + source - admit * flux)
            fluxes.append(flux)
        net_ref[LEV : LEV + 1, :] = jnp.sum(total, axis=0, keepdims=True)

        def upward(step, fluxes):
            for odd in range(4):
                layer = LEV - 1 - 4 * step - odd
                total = down_ref[layer]
                out = []
                for g in range(GB):
                    rows = pl.ds(g * SUB, SUB)
                    flux = gain_ref[layer, rows, :] * fluxes[g] + add_ref[layer, rows, :]
                    total = total - admit_ref[layer, rows, :] * flux
                    out.append(flux)
                fluxes = tuple(out)
                net_ref[pl.ds(layer, 1), :] = jnp.sum(total, axis=0, keepdims=True)
            return fluxes

        lax.fori_loop(0, LEV // 4, upward, tuple(fluxes))
        live = map_ref[:, lanes] >= 0
        result_ref[:, lanes] = jnp.where(live, net_ref[0:LEV, :] - net_ref[1 : LEV + 1, :], 0.0)
        return carry

    lax.fori_loop(0, 2, one_block, 0)
    out_copy = pltpu.make_async_copy(result_ref, out_hbm, out_sem.at[0])
    out_copy.start()

    member = member_ref[...]
    slots = member.shape[1]
    absorbed = jnp.concatenate([result_ref[...], jnp.zeros((LANES - LEV, slots), f32)], axis=0)
    high = absorbed.astype(bf16)
    low = (absorbed - high.astype(f32)).astype(bf16)
    part_ref[...] = (mxu(member, high, NT) + mxu(member, low, NT)).reshape(2, chips, LANES)

    copy = remote(part_ref.at[1 - core], other_ref, send_b, recv_b, 1, sibling)
    copy.start()
    copy.wait()
    strip_ref[...] = (part_ref[core] + other_ref[...]).reshape(chips, 1, LANES)
    copies = [
        remote(strip_ref.at[lax.div(device[0], 2) * n_lat + device[1]], last_ref.at[n], send_c, recv_c, n, device)
        for n, device in enumerate(peers)
    ]
    for copy in copies:
        copy.start()
    for copy in copies:
        copy.wait()
    total = strip_ref[chip] + jnp.sum(last_ref[...], axis=0)
    mean_ref[...] = total[:, :LEV] * (1.0 / LANES)
    out_copy.wait()


def columns_absorbed(features, cosine, albedo, sunlit, column_map, swap_list, gas_table, asymmetry, solar):
    anywhere = pl.BlockSpec(memory_space=pl.ANY)
    vmem = pl.BlockSpec(memory_space=pltpu.VMEM)
    f32, bf16, i32 = jnp.float32, jnp.bfloat16, jnp.int32
    chips = lax.axis_size("lon") * lax.axis_size("lat") // 2
    dma = pltpu.SemaphoreType.DMA
    return pl.pallas_call(
        column_kernel,
        out_shape=(jax.ShapeDtypeStruct((LEV, 2 * LANES), f32), jax.ShapeDtypeStruct((1, LEV), f32)),
        in_specs=[anywhere] * 9,
        out_specs=(anywhere, vmem),
        scratch_shapes=[
            pltpu.VMEM((2 * LANES, LEV * NF), bf16),
            pltpu.VMEM((2 * LANES,), bf16),
            pltpu.VMEM((2, 2 * LANES), bf16),
            pltpu.VMEM((1, 2 * LANES), i32),
            pltpu.VMEM((1, 2 * LANES), i32),
            pltpu.VMEM((NF, 2 * G), bf16),
            pltpu.VMEM((1, G), f32),
            pltpu.VMEM((1, G), f32),
            pltpu.VMEM((1, LANES // 2), i32),
            pltpu.VMEM((KINDS * G, LANES), bf16),
            pltpu.VMEM((3, G, LANES), f32),
            pltpu.VMEM((G, LANES), f32),
            pltpu.VMEM((KINDS * G, 2 * LANES), f32),
            pltpu.VMEM((KINDS * G, 2 * LANES), f32),
            pltpu.VMEM((KINDS * G, 2 * LANES), f32),
            pltpu.VMEM((KINDS * G, 2 * LANES), f32),
            pltpu.VMEM((KINDS * G, 2 * LANES), f32),
            pltpu.VMEM((KINDS * G, 2 * LANES), f32),
            pltpu.VMEM((KINDS * G, 2 * LANES), f32),
            pltpu.VMEM((KINDS * G, 2 * LANES), f32),
            pltpu.VMEM((4, G, LANES), f32),
            pltpu.VMEM((LEV, G, LANES), f32),
            pltpu.VMEM((LEV, G, LANES), f32),
            pltpu.VMEM((LEV, G, LANES), f32),
            pltpu.VMEM((LEV, SUB, LANES), f32),
            pltpu.VMEM((LEV + SUB, LANES), f32),
            pltpu.VMEM((1, 2 * LANES), f32),
            pltpu.VMEM((LEV, 2 * LANES), f32),
            pltpu.VMEM((2 * chips, 2 * LANES), bf16),
            pltpu.VMEM((1, 1, LANES), f32),
            pltpu.VMEM((2, chips, 1, LANES), f32),
            pltpu.VMEM((2, chips, LANES), f32),
            pltpu.VMEM((chips, LANES), f32),
            pltpu.VMEM((chips, 1, LANES), f32),
            pltpu.VMEM((chips - 1, 1, LANES), f32),
            dma((8,)), dma((2,)), dma((2,)), dma((chips,)), dma((chips,)), dma((2,)), dma((2,)), dma((chips,)), dma((chips,)),
        ],
        compiler_params=pltpu.CompilerParams(collective_id=0, has_side_effects=True, vmem_limit_bytes=60 * 1024 * 1024),
        cost_estimate=pl.CostEstimate(flops=200_000_000, bytes_accessed=2_200_000, transcendentals=10_000_000),
    )(features, cosine, albedo, sunlit[None], column_map[None], gas_table, asymmetry[None], solar[None], swap_list[None])

def body(
    features, cosine_zenith, albedo, sunlit, column_map, swap_list, gas_table, asymmetry, solar_source
):
    return columns_absorbed(
        features, cosine_zenith, albedo, sunlit, column_map, swap_list, gas_table, asymmetry, solar_source
    )


def solution(mesh):
    both = ("lon", "lat")
    in_specs = (
        P(both, None), P(both), P(None, both), P(both), P(both), P(both), P(), P(), P(),
    )
    out_specs = (P(None, both), P(both, None))
    return jax.shard_map(body, mesh=mesh, in_specs=in_specs, out_specs=out_specs, check_vma=False)
```

```python
import functools
import jax
import jax.numpy as jnp
from jax import lax
from jax.sharding import PartitionSpec as P
from jax.experimental import pallas as pl
from jax.experimental.pallas import tpu as pltpu

LEV = 64
NF = 64
G = 112
LANES = 128
SUB = 8
GB = G // SUB
PAIRS = LEV // 2
KINDS = 2
LOG2E = 1.4426950408889634
NT = (((1,), (1,)), ((), ()))
NN = (((1,), (0,)), ((), ()))


def recip(x):
    return pl.reciprocal(x, approx=True)


def mxu(a, b, dims):
    return lax.dot_general(a, b, dims, preferred_element_type=jnp.float32)


def column_kernel(
    feat_hbm, cosine_hbm, albedo_hbm, sunlit_hbm, map_hbm, gas_hbm, asym_hbm, solar_hbm, swap_hbm,
    result_ref, mean_ref,
    feat_ref, cosine_ref, albedo_ref, sunlit_ref, map_ref, gas_ref, asym_ref, solar_ref, swap_ref,
    weight_ref, const_ref, solar_rows_ref, depth_0, depth_1, depth_2, depth_3, depth_4, depth_5, depth_6, depth_7,
    state_ref, gain_ref, add_ref, admit_ref, down_ref, net_ref,
    wide_ref, member_ref, own_ref, mask_ref, part_ref, other_ref, strip_ref, last_ref,
    small_sem, feat_sem, send_a, recv_a, send_b, recv_b, send_c, recv_c,
):
    f32 = jnp.float32
    bf16 = jnp.bfloat16
    chunks = [
        pltpu.make_async_copy(
            feat_hbm.at[pl.ds(n * LANES, LANES), :], feat_ref.at[pl.ds(n * LANES, LANES), :], feat_sem.at[n]
        )
        for n in range(2)
    ]
    small = [
        pltpu.make_async_copy(src, dst, small_sem.at[n])
        for n, (src, dst) in enumerate(
            (
                (sunlit_hbm, sunlit_ref), (map_hbm, map_ref), (cosine_hbm, cosine_ref),
                (albedo_hbm, albedo_ref), (gas_hbm, gas_ref), (asym_hbm, asym_ref), (solar_hbm, solar_ref),
                (swap_hbm, swap_ref),
            )
        )
    ]
    for copy in chunks:
        copy.start()
    for copy in small:
        copy.start()

    n_lon, n_lat = lax.axis_size("lon"), lax.axis_size("lat")
    lon, lat = lax.axis_index("lon"), lax.axis_index("lat")
    groups = n_lon * n_lat
    chips = groups // 2
    core = lax.rem(lon, 2)
    chip = lax.div(lon, 2) * n_lat + lat
    mesh_ids = pl.DeviceIdType.MESH
    sibling = (lon + 1 - 2 * core, lat)
    n_x, n_z = n_lon // 4, n_lat // 2
    steps = [
        (dx, high, dz, low_bit)
        for dx in range(n_x) for high in range(2) for dz in range(n_z) for low_bit in range(2)
        if dx or high or dz or low_bit
    ]
    steps.sort(key=lambda d: -(min(d[0], n_x - d[0]) + min(d[2], n_z - d[2]) + (1 if d[3] else 2 * d[1])))
    x, y_high = lax.div(lon, 4), lax.rem(lax.div(lon, 2), 2)
    z, y_low = lax.div(lat, 2), lax.rem(lat, 2)
    peers = [
        (
            lax.rem(x + dx, n_x) * 4 + lax.rem(y_high + high, 2) * 2 + core,
            lax.rem(z + dz, n_z) * 2 + lax.rem(y_low + low_bit, 2),
        )
        for dx, high, dz, low_bit in steps
    ]
    barrier = pltpu.get_barrier_semaphore()
    for device in [sibling] + peers:
        pl.semaphore_signal(barrier, inc=1, device_id=device, device_id_type=mesh_ids)

    def remote(src, dst, sends, recvs, n, device):
        return pltpu.make_async_remote_copy(
            src_ref=src, dst_ref=dst, send_sem=sends.at[n], recv_sem=recvs.at[n],
            device_id=device, device_id_type=mesh_ids,
        )

    mask_copies = [
        remote(own_ref.at[0], mask_ref.at[core, chip], send_a, recv_a, n, device)
        for n, device in enumerate(peers)
    ]
    mask_pair = remote(mask_ref.at[core], mask_ref.at[core], send_b, recv_b, 0, sibling)

    for copy in small:
        copy.wait()

    listed = jnp.broadcast_to(swap_ref[...].astype(f32), (LANES, LANES // 2)).T
    lane_no = lax.broadcasted_iota(jnp.int32, (LANES // 2, LANES), 1).astype(f32)
    own_ref[0] = jnp.max(jnp.where(listed == lane_no, 1.0, 0.0), axis=0, keepdims=True)

    wide_ref[...] = jnp.reshape(cosine_ref[...].astype(f32), (1, 2 * LANES))
    table = gas_ref[...]
    stacked = jnp.concatenate([table, table], axis=0)
    row = lax.broadcasted_iota(jnp.int32, (2 * G, 2 * G), 0)
    col = lax.broadcasted_iota(jnp.int32, (2 * G, 2 * G), 1)
    turned = mxu(jnp.where(row == col, 1.0, 0.0).astype(bf16), stacked, NT)

    def to_rows(line):
        return jnp.broadcast_to(line, (LANES, G)).T

    asym = to_rows(asym_ref[...])
    solar_rows_ref[...] = to_rows(solar_ref[...])
    absorb = turned[:G]
    scatter = turned[G:]
    first = lax.broadcasted_iota(jnp.int32, (G, LANES), 1) < NF
    weight_ref[:G, :] = jnp.where(first, 2.0 * absorb, 2.0 * scatter).astype(bf16)
    weight_ref[G:, :] = jnp.where(first, 0.0, 2.0 * scatter).astype(bf16)
    const_ref[0] = 0.245 * (1.0 + 3.0 * asym)
    const_ref[1] = 0.98 * (0.5 - 0.25 * asym)
    const_ref[2] = 0.98 * (0.5 + 0.25 * asym)

    low_lanes = lax.broadcasted_iota(jnp.int32, (LANES, LANES), 1) < NF

    def one_block(block, carry):
        @pl.when(block == 0)
        def _():
            chunks[0].wait()

        @pl.when(block == 1)
        def _():
            chunks[1].wait()

        lanes = pl.ds(pl.multiple_of(block * LANES, LANES), LANES)
        cosine = wide_ref[:, lanes]
        slant = jnp.broadcast_to((-0.5 * LOG2E) / cosine, (SUB, LANES))
        alb_dir = jnp.broadcast_to(albedo_ref[0:1, lanes].astype(f32), (SUB, LANES))
        alb_dif = jnp.broadcast_to(albedo_ref[1:2, lanes].astype(f32), (SUB, LANES))
        state_ref[0] = solar_rows_ref[...] * (cosine * sunlit_ref[:, lanes].astype(f32))
        state_ref[1] = jnp.ones((G, LANES), f32)
        state_ref[2] = jnp.zeros((G, LANES), f32)
        state_ref[3] = jnp.zeros((G, LANES), f32)

        def optical(pair, depth, guard=None):
            chunk = feat_ref[lanes, pl.ds(pl.multiple_of(pair * LANES, LANES), LANES)]
            if guard is not None:
                chunk = chunk + guard
            turn = chunk.T
            both = jnp.concatenate(
                [
                    jnp.concatenate([turn[:NF], turn[:NF]], axis=0),
                    jnp.concatenate([turn[NF:], turn[NF:]], axis=0),
                ],
                axis=1,
            )
            depth[...] = mxu(weight_ref[...], both, NN)

        def one_pair(pair, depth):
            totals = [jnp.zeros((SUB, LANES), f32) for _ in range(2)]
            for g in range(GB):
                rows = pl.ds(g * SUB, SUB)
                direct, admit, source, left = (state_ref[n, rows, :] for n in range(4))
                slope, to_up, to_dn = (const_ref[n, rows, :] for n in range(3))
                for odd in range(2):
                    layer = 2 * pair + odd
                    tau, ray = (
                        depth[n * G + g * SUB : n * G + (g + 1) * SUB, odd * LANES : (odd + 1) * LANES]
                        for n in range(KINDS)
                    )
                    t_one = tau - 0.98 * ray
                    t_two = tau - slope * ray
                    product = t_one * t_two
                    root = lax.rsqrt(product)
                    x = product * root
                    sigma = t_one * root
                    th = jnp.tanh(x)
                    e = jnp.exp2(x * (-LOG2E))
                    sech = e + e * th
                    below = direct * jnp.exp2(tau * slant)
                    lost = (direct - below) * recip(tau) * ray
                    up = to_up * lost
                    dn = to_dn * lost
                    jump = up - left
                    totals[odd] = totals[odd] + (source + direct)
                    inner = source + up - admit * jump
                    z = recip(sigma + admit * th)
                    zs = z * sigma
                    gain = sech * zs
                    gain_ref[layer, rows, :] = gain
                    add_ref[layer, rows, :] = (th * z) * inner + jump
                    admit_ref[layer, rows, :] = admit
                    admit = (admit + sigma * th) * zs
                    source = gain * inner + dn
                    direct = below
                    left = dn
                for n, value in enumerate((direct, admit, source, left)):
                    state_ref[n, rows, :] = value
            for odd in range(2):
                down_ref[2 * pair + odd] = totals[odd]
            return jnp.minimum(th[0:1], 0.0).astype(bf16)

        optical(0, depth_0)
        optical(1, depth_1)
        optical(2, depth_2)
        optical(3, depth_3)

        def down(step, inner_carry):
            @pl.when((block == 0) & (step == PAIRS // 8 - 1))
            def _():
                pl.semaphore_wait(barrier, chips)
                mask_ref[core, chip] = own_ref[0]
                for copy in mask_copies:
                    copy.start()

            @pl.when((block == 1) & (step == PAIRS // 8 - 1))
            def _():
                for copy in mask_copies:
                    copy.wait()
                mask_pair.start()

            guard = None
            next_guard = one_pair(8 * step + 0, depth_0)
            optical(8 * step + 4, depth_4, guard)
            guard = next_guard
            next_guard = one_pair(8 * step + 1, depth_1)
            optical(8 * step + 5, depth_5, guard)
            guard = next_guard
            next_guard = one_pair(8 * step + 2, depth_2)
            optical(8 * step + 6, depth_6, guard)
            guard = next_guard
            next_guard = one_pair(8 * step + 3, depth_3)
            optical(8 * step + 7, depth_7, guard)
            guard = next_guard
            next_guard = one_pair(8 * step + 4, depth_4)
            optical(jnp.minimum(8 * step + 8, PAIRS - 1), depth_0, guard)
            guard = next_guard
            next_guard = one_pair(8 * step + 5, depth_5)
            optical(jnp.minimum(8 * step + 9, PAIRS - 1), depth_1, guard)
            guard = next_guard
            next_guard = one_pair(8 * step + 6, depth_6)
            optical(jnp.minimum(8 * step + 10, PAIRS - 1), depth_2, guard)
            guard = next_guard
            next_guard = one_pair(8 * step + 7, depth_7)
            optical(jnp.minimum(8 * step + 11, PAIRS - 1), depth_3, guard)
            guard = next_guard
            return inner_carry

        lax.fori_loop(0, PAIRS // 8, down, 0)

        @pl.when(block == 1)
        def _():
            mask_pair.wait()

            place = map_ref[...]
            home = lax.shift_right_arithmetic(place, 7)
            home_core = lax.rem(lax.div(home, n_lat), 2)
            home_chip = lax.div(home, 2 * n_lat) * n_lat + lax.rem(home, n_lat)
            away_chip = jnp.where(home_chip >= chips // 2, home_chip - chips // 2, home_chip + chips // 2)
            slot = place & (LANES - 1)
            slots = place.shape[1]
            group_row = lax.broadcasted_iota(jnp.int32, (groups, slots), 0)
            at_home = jnp.where(home_core * chips + home_chip == group_row, 1.0, 0.0).astype(bf16)
            at_slot = jnp.where(slot == lax.broadcasted_iota(jnp.int32, (LANES, slots), 0), 1.0, 0.0)
            masks = mask_ref[...].reshape(groups, LANES)
            listed_at = mxu(masks.T.astype(bf16), at_home, NN)
            moved = jnp.sum(listed_at * at_slot, axis=0, keepdims=True)
            held = home_core * chips + jnp.where(moved > 0.5, away_chip, home_chip)
            held = jnp.where(place < 0, -1, held)
            member_ref[...] = jnp.where(held == group_row, 1.0, 0.0).astype(bf16)

        fluxes = []
        total = jnp.zeros((SUB, LANES), f32)
        for g in range(GB):
            rows = pl.ds(g * SUB, SUB)
            direct, admit, source, left = (state_ref[n, rows, :] for n in range(4))
            over = source * (1.0 + alb_dif) + 2.0 * alb_dir * direct - left * (1.0 - alb_dif)
            flux = over / ((1.0 - alb_dif) + admit * (1.0 + alb_dif))
            total = total + (direct + source - admit * flux)
            fluxes.append(flux)
        net_ref[LEV : LEV + 1, :] = jnp.sum(total, axis=0, keepdims=True)

        def upward(step, fluxes):
            for odd in range(4):
                layer = LEV - 1 - 4 * step - odd
                total = down_ref[layer]
                out = []
                for g in range(GB):
                    rows = pl.ds(g * SUB, SUB)
                    flux = gain_ref[layer, rows, :] * fluxes[g] + add_ref[layer, rows, :]
                    total = total - admit_ref[layer, rows, :] * flux
                    out.append(flux)
                fluxes = tuple(out)
                net_ref[pl.ds(layer, 1), :] = jnp.sum(total, axis=0, keepdims=True)
            return fluxes

        lax.fori_loop(0, LEV // 4, upward, tuple(fluxes))
        live = map_ref[:, lanes] >= 0
        result_ref[:, lanes] = jnp.where(live, net_ref[0:LEV, :] - net_ref[1 : LEV + 1, :], 0.0)
        return carry

    lax.fori_loop(0, 2, one_block, 0)

    member = member_ref[...]
    slots = member.shape[1]
    absorbed = jnp.concatenate([result_ref[...], jnp.zeros((LANES - LEV, slots), f32)], axis=0)
    high = absorbed.astype(bf16)
    low = (absorbed - high.astype(f32)).astype(bf16)
    part_ref[...] = (mxu(member, high, NT) + mxu(member, low, NT)).reshape(2, chips, LANES)

    copy = remote(part_ref.at[1 - core], other_ref, send_b, recv_b, 1, sibling)
    copy.start()
    copy.wait()
    strip_ref[...] = (part_ref[core] + other_ref[...]).reshape(chips, 1, LANES)
    copies = [
        remote(strip_ref.at[lax.div(device[0], 2) * n_lat + device[1]], last_ref.at[n], send_c, recv_c, n, device)
        for n, device in enumerate(peers)
    ]
    for copy in copies:
        copy.start()
    for copy in copies:
        copy.wait()
    total = strip_ref[chip] + jnp.sum(last_ref[...], axis=0)
    mean_ref[...] = total[:, :LEV] * (1.0 / LANES)


def columns_absorbed(features, cosine, albedo, sunlit, column_map, swap_list, gas_table, asymmetry, solar):
    anywhere = pl.BlockSpec(memory_space=pl.ANY)
    vmem = pl.BlockSpec(memory_space=pltpu.VMEM)
    f32, bf16, i32 = jnp.float32, jnp.bfloat16, jnp.int32
    chips = lax.axis_size("lon") * lax.axis_size("lat") // 2
    dma = pltpu.SemaphoreType.DMA
    return pl.pallas_call(
        column_kernel,
        out_shape=(pltpu.VMEM((LEV, 2 * LANES), f32), pltpu.VMEM((1, LEV), f32)),
        in_specs=[anywhere] * 9,
        out_specs=(vmem, vmem),
        scratch_shapes=[
            pltpu.VMEM((2 * LANES, LEV * NF), bf16),
            pltpu.VMEM((2 * LANES,), bf16),
            pltpu.VMEM((2, 2 * LANES), bf16),
            pltpu.VMEM((1, 2 * LANES), i32),
            pltpu.VMEM((1, 2 * LANES), i32),
            pltpu.VMEM((NF, 2 * G), bf16),
            pltpu.VMEM((1, G), f32),
            pltpu.VMEM((1, G), f32),
            pltpu.VMEM((1, LANES // 2), i32),
            pltpu.VMEM((KINDS * G, LANES), bf16),
            pltpu.VMEM((3, G, LANES), f32),
            pltpu.VMEM((G, LANES), f32),
            pltpu.VMEM((KINDS * G, 2 * LANES), f32),
            pltpu.VMEM((KINDS * G, 2 * LANES), f32),
            pltpu.VMEM((KINDS * G, 2 * LANES), f32),
            pltpu.VMEM((KINDS * G, 2 * LANES), f32),
            pltpu.VMEM((KINDS * G, 2 * LANES), f32),
            pltpu.VMEM((KINDS * G, 2 * LANES), f32),
            pltpu.VMEM((KINDS * G, 2 * LANES), f32),
            pltpu.VMEM((KINDS * G, 2 * LANES), f32),
            pltpu.VMEM((4, G, LANES), f32),
            pltpu.VMEM((LEV, G, LANES), f32),
            pltpu.VMEM((LEV, G, LANES), f32),
            pltpu.VMEM((LEV, G, LANES), f32),
            pltpu.VMEM((LEV, SUB, LANES), f32),
            pltpu.VMEM((LEV + SUB, LANES), f32),
            pltpu.VMEM((1, 2 * LANES), f32),
            pltpu.VMEM((2 * chips, 2 * LANES), bf16),
            pltpu.VMEM((1, 1, LANES), f32),
            pltpu.VMEM((2, chips, 1, LANES), f32),
            pltpu.VMEM((2, chips, LANES), f32),
            pltpu.VMEM((chips, LANES), f32),
            pltpu.VMEM((chips, 1, LANES), f32),
            pltpu.VMEM((chips - 1, 1, LANES), f32),
            dma((8,)), dma((2,)), dma((chips,)), dma((chips,)), dma((2,)), dma((2,)), dma((chips,)), dma((chips,)),
        ],
        compiler_params=pltpu.CompilerParams(collective_id=0, has_side_effects=True, vmem_limit_bytes=60 * 1024 * 1024),
        cost_estimate=pl.CostEstimate(flops=200_000_000, bytes_accessed=2_200_000, transcendentals=10_000_000),
    )(features, cosine, albedo, sunlit[None], column_map[None], gas_table, asymmetry[None], solar[None], swap_list[None])

def body(
    features, cosine_zenith, albedo, sunlit, column_map, swap_list, gas_table, asymmetry, solar_source
):
    return columns_absorbed(
        features, cosine_zenith, albedo, sunlit, column_map, swap_list, gas_table, asymmetry, solar_source
    )


def solution(mesh):
    both = ("lon", "lat")
    in_specs = (
        P(both, None), P(both), P(None, both), P(both), P(both), P(both), P(), P(), P(),
    )
    out_specs = (P(None, both), P(both, None))
    return jax.shard_map(body, mesh=mesh, in_specs=in_specs, out_specs=out_specs, check_vma=False)
```

```python
import functools
import jax
import jax.numpy as jnp
from jax import lax
from jax.sharding import PartitionSpec as P
from jax.experimental import pallas as pl
from jax.experimental.pallas import tpu as pltpu

LEV = 64
NF = 64
G = 112
LANES = 128
SUB = 8
GB = G // SUB
PAIRS = LEV // 2
KINDS = 2
LOG2E = 1.4426950408889634
NT = (((1,), (1,)), ((), ()))
NN = (((1,), (0,)), ((), ()))


def recip(x):
    return pl.reciprocal(x, approx=True)


def mxu(a, b, dims):
    return lax.dot_general(a, b, dims, preferred_element_type=jnp.float32)


def column_kernel(
    feat_hbm, cosine_hbm, albedo_hbm, sunlit_hbm, map_hbm, gas_hbm, asym_hbm, solar_hbm, swap_hbm,
    result_ref, mean_ref,
    feat_ref, cosine_ref, albedo_ref, sunlit_ref, map_ref, gas_ref, asym_ref, solar_ref, swap_ref,
    weight_ref, const_ref, solar_rows_ref, depth_0, depth_1, depth_2, depth_3, depth_4, depth_5, depth_6, depth_7,
    state_ref, gain_ref, add_ref, admit_ref, down_ref, net_ref,
    wide_ref, member_ref, own_ref, mask_ref, part_ref, other_ref, strip_ref, last_ref,
    small_sem, feat_sem, send_a, recv_a, send_b, recv_b, send_c, recv_c,
):
    f32 = jnp.float32
    bf16 = jnp.bfloat16
    chunks = [
        pltpu.make_async_copy(
            feat_hbm.at[pl.ds(n * LANES, LANES), :], feat_ref.at[pl.ds(n * LANES, LANES), :], feat_sem.at[n]
        )
        for n in range(2)
    ]
    small = [
        pltpu.make_async_copy(src, dst, small_sem.at[n])
        for n, (src, dst) in enumerate(
            (
                (sunlit_hbm, sunlit_ref), (map_hbm, map_ref), (cosine_hbm, cosine_ref),
                (albedo_hbm, albedo_ref), (gas_hbm, gas_ref), (asym_hbm, asym_ref), (solar_hbm, solar_ref),
                (swap_hbm, swap_ref),
            )
        )
    ]
    for copy in chunks:
        copy.start()
    for copy in small:
        copy.start()

    n_lon, n_lat = lax.axis_size("lon"), lax.axis_size("lat")
    lon, lat = lax.axis_index("lon"), lax.axis_index("lat")
    groups = n_lon * n_lat
    chips = groups // 2
    core = lax.rem(lon, 2)
    chip = lax.div(lon, 2) * n_lat + lat
    mesh_ids = pl.DeviceIdType.MESH
    sibling = (lon + 1 - 2 * core, lat)
    n_x, n_z = n_lon // 4, n_lat // 2
    steps = [
        (dx, high, dz, low_bit)
        for dx in range(n_x) for high in range(2) for dz in range(n_z) for low_bit in range(2)
        if dx or high or dz or low_bit
    ]
    steps.sort(key=lambda d: -(min(d[0], n_x - d[0]) + min(d[2], n_z - d[2]) + (1 if d[3] else 2 * d[1])))
    x, y_high = lax.div(lon, 4), lax.rem(lax.div(lon, 2), 2)
    z, y_low = lax.div(lat, 2), lax.rem(lat, 2)
    peers = [
        (
            lax.rem(x + dx, n_x) * 4 + lax.rem(y_high + high, 2) * 2 + core,
            lax.rem(z + dz, n_z) * 2 + lax.rem(y_low + low_bit, 2),
        )
        for dx, high, dz, low_bit in steps
    ]
    barrier = pltpu.get_barrier_semaphore()
    for device in [sibling] + peers:
        pl.semaphore_signal(barrier, inc=1, device_id=device, device_id_type=mesh_ids)

    def remote(src, dst, sends, recvs, n, device):
        return pltpu.make_async_remote_copy(
            src_ref=src, dst_ref=dst, send_sem=sends.at[n], recv_sem=recvs.at[n],
            device_id=device, device_id_type=mesh_ids,
        )

    mask_copies = [
        remote(own_ref.at[0], mask_ref.at[core, chip], send_a, recv_a, n, device)
        for n, device in enumerate(peers)
    ]
    mask_pair = remote(mask_ref.at[core], mask_ref.at[core], send_b, recv_b, 0, sibling)

    for copy in small:
        copy.wait()

    listed = jnp.broadcast_to(swap_ref[...].astype(f32), (LANES, LANES // 2)).T
    lane_no = lax.broadcasted_iota(jnp.int32, (LANES // 2, LANES), 1).astype(f32)
    own_ref[0] = jnp.max(jnp.where(listed == lane_no, 1.0, 0.0), axis=0, keepdims=True)

    wide_ref[...] = jnp.reshape(cosine_ref[...].astype(f32), (1, 2 * LANES))
    table = gas_ref[...]
    stacked = jnp.concatenate([table, table], axis=0)
    row = lax.broadcasted_iota(jnp.int32, (2 * G, 2 * G), 0)
    col = lax.broadcasted_iota(jnp.int32, (2 * G, 2 * G), 1)
    turned = mxu(jnp.where(row == col, 1.0, 0.0).astype(bf16), stacked, NT)

    def to_rows(line):
        return jnp.broadcast_to(line, (LANES, G)).T

    asym = to_rows(asym_ref[...])
    solar_rows_ref[...] = to_rows(solar_ref[...])
    absorb = turned[:G]
    scatter = turned[G:]
    first = lax.broadcasted_iota(jnp.int32, (G, LANES), 1) < NF
    weight_ref[:G, :] = jnp.where(first, 2.0 * absorb, 2.0 * scatter).astype(bf16)
    weight_ref[G:, :] = jnp.where(first, 0.0, 2.0 * scatter).astype(bf16)
    const_ref[0] = 0.245 * (1.0 + 3.0 * asym)
    const_ref[1] = 0.98 * (0.5 - 0.25 * asym)
    const_ref[2] = 0.98 * (0.5 + 0.25 * asym)

    low_lanes = lax.broadcasted_iota(jnp.int32, (LANES, LANES), 1) < NF

    def one_block(block, carry):
        @pl.when(block == 0)
        def _():
            chunks[0].wait()

        @pl.when(block == 1)
        def _():
            chunks[1].wait()

        lanes = pl.ds(pl.multiple_of(block * LANES, LANES), LANES)
        cosine = wide_ref[:, lanes]
        slant = jnp.broadcast_to((-0.5 * LOG2E) / cosine, (SUB, LANES))
        alb_dir = jnp.broadcast_to(albedo_ref[0:1, lanes].astype(f32), (SUB, LANES))
        alb_dif = jnp.broadcast_to(albedo_ref[1:2, lanes].astype(f32), (SUB, LANES))
        state_ref[0] = solar_rows_ref[...] * (cosine * sunlit_ref[:, lanes].astype(f32))
        state_ref[1] = jnp.ones((G, LANES), f32)
        state_ref[2] = jnp.zeros((G, LANES), f32)
        state_ref[3] = jnp.zeros((G, LANES), f32)

        def optical(pair, depth, guard=None):
            chunk = feat_ref[lanes, pl.ds(pl.multiple_of(pair * LANES, LANES), LANES)]
            if guard is not None:
                chunk = chunk + guard
            turn = chunk.T
            both = jnp.concatenate(
                [
                    jnp.concatenate([turn[:NF], turn[:NF]], axis=0),
                    jnp.concatenate([turn[NF:], turn[NF:]], axis=0),
                ],
                axis=1,
            )
            depth[...] = mxu(weight_ref[...], both, NN)

        def one_pair(pair, depth):
            totals = [jnp.zeros((SUB, LANES), f32) for _ in range(2)]
            for g in range(GB):
                rows = pl.ds(g * SUB, SUB)
                direct, admit, source, left = (state_ref[n, rows, :] for n in range(4))
                slope, to_up, to_dn = (const_ref[n, rows, :] for n in range(3))
                for odd in range(2):
                    layer = 2 * pair + odd
                    tau, ray = (
                        depth[n * G + g * SUB : n * G + (g + 1) * SUB, odd * LANES : (odd + 1) * LANES]
                        for n in range(KINDS)
                    )
                    t_one = tau - 0.98 * ray
                    t_two = tau - slope * ray
                    root = lax.rsqrt(t_two)
                    first_root = t_one * lax.rsqrt(t_one)
                    x = first_root * (t_two * root)
                    sigma = first_root * root
                    th = jnp.tanh(x)
                    e = jnp.exp2(x * (-LOG2E))
                    sech = e + e * th
                    below = direct * jnp.exp2(tau * slant)
                    lost = (direct - below) * recip(tau) * ray
                    up = to_up * lost
                    dn = to_dn * lost
                    jump = up - left
                    totals[odd] = totals[odd] + (source + direct)
                    inner = source + up - admit * jump
                    z = recip(sigma + admit * th)
                    zs = z * sigma
                    gain = sech * zs
                    gain_ref[layer, rows, :] = gain
                    add_ref[layer, rows, :] = (th * z) * inner + jump
                    admit_ref[layer, rows, :] = admit
                    admit = (admit + sigma * th) * zs
                    source = gain * inner + dn
                    direct = below
                    left = dn
                for n, value in enumerate((direct, admit, source, left)):
                    state_ref[n, rows, :] = value
            for odd in range(2):
                down_ref[2 * pair + odd] = totals[odd]
            return jnp.minimum(th[0:1], 0.0).astype(bf16)

        optical(0, depth_0)
        optical(1, depth_1)
        optical(2, depth_2)
        optical(3, depth_3)

        def down(step, inner_carry):
            @pl.when((block == 0) & (step == PAIRS // 8 - 1))
            def _():
                pl.semaphore_wait(barrier, chips)
                mask_ref[core, chip] = own_ref[0]
                for copy in mask_copies:
                    copy.start()

            @pl.when((block == 1) & (step == PAIRS // 8 - 1))
            def _():
                for copy in mask_copies:
                    copy.wait()
                mask_pair.start()

            guard = None
            next_guard = one_pair(8 * step + 0, depth_0)
            optical(8 * step + 4, depth_4, guard)
            guard = next_guard
            next_guard = one_pair(8 * step + 1, depth_1)
            optical(8 * step + 5, depth_5, guard)
            guard = next_guard
            next_guard = one_pair(8 * step + 2, depth_2)
            optical(8 * step + 6, depth_6, guard)
            guard = next_guard
            next_guard = one_pair(8 * step + 3, depth_3)
            optical(8 * step + 7, depth_7, guard)
            guard = next_guard
            next_guard = one_pair(8 * step + 4, depth_4)
            optical(jnp.minimum(8 * step + 8, PAIRS - 1), depth_0, guard)
            guard = next_guard
            next_guard = one_pair(8 * step + 5, depth_5)
            optical(jnp.minimum(8 * step + 9, PAIRS - 1), depth_1, guard)
            guard = next_guard
            next_guard = one_pair(8 * step + 6, depth_6)
            optical(jnp.minimum(8 * step + 10, PAIRS - 1), depth_2, guard)
            guard = next_guard
            next_guard = one_pair(8 * step + 7, depth_7)
            optical(jnp.minimum(8 * step + 11, PAIRS - 1), depth_3, guard)
            guard = next_guard
            return inner_carry

        lax.fori_loop(0, PAIRS // 8, down, 0)

        @pl.when(block == 1)
        def _():
            mask_pair.wait()

            place = map_ref[...]
            home = lax.shift_right_arithmetic(place, 7)
            home_core = lax.rem(lax.div(home, n_lat), 2)
            home_chip = lax.div(home, 2 * n_lat) * n_lat + lax.rem(home, n_lat)
            away_chip = jnp.where(home_chip >= chips // 2, home_chip - chips // 2, home_chip + chips // 2)
            slot = place & (LANES - 1)
            slots = place.shape[1]
            group_row = lax.broadcasted_iota(jnp.int32, (groups, slots), 0)
            at_home = jnp.where(home_core * chips + home_chip == group_row, 1.0, 0.0).astype(bf16)
            at_slot = jnp.where(slot == lax.broadcasted_iota(jnp.int32, (LANES, slots), 0), 1.0, 0.0)
            masks = mask_ref[...].reshape(groups, LANES)
            listed_at = mxu(masks.T.astype(bf16), at_home, NN)
            moved = jnp.sum(listed_at * at_slot, axis=0, keepdims=True)
            held = home_core * chips + jnp.where(moved > 0.5, away_chip, home_chip)
            held = jnp.where(place < 0, -1, held)
            member_ref[...] = jnp.where(held == group_row, 1.0, 0.0).astype(bf16)

        fluxes = []
        total = jnp.zeros((SUB, LANES), f32)
        for g in range(GB):
            rows = pl.ds(g * SUB, SUB)
            direct, admit, source, left = (state_ref[n, rows, :] for n in range(4))
            over = source * (1.0 + alb_dif) + 2.0 * alb_dir * direct - left * (1.0 - alb_dif)
            flux = over / ((1.0 - alb_dif) + admit * (1.0 + alb_dif))
            total = total + (direct + source - admit * flux)
            fluxes.append(flux)
        net_ref[LEV : LEV + 1, :] = jnp.sum(total, axis=0, keepdims=True)

        def upward(step, fluxes):
            for odd in range(4):
                layer = LEV - 1 - 4 * step - odd
                total = down_ref[layer]
                out = []
                for g in range(GB):
                    rows = pl.ds(g * SUB, SUB)
                    flux = gain_ref[layer, rows, :] * fluxes[g] + add_ref[layer, rows, :]
                    total = total - admit_ref[layer, rows, :] * flux
                    out.append(flux)
                fluxes = tuple(out)
                net_ref[pl.ds(layer, 1), :] = jnp.sum(total, axis=0, keepdims=True)
            return fluxes

        lax.fori_loop(0, LEV // 4, upward, tuple(fluxes))
        live = map_ref[:, lanes] >= 0
        result_ref[:, lanes] = jnp.where(live, net_ref[0:LEV, :] - net_ref[1 : LEV + 1, :], 0.0)
        return carry

    lax.fori_loop(0, 2, one_block, 0)

    member = member_ref[...]
    slots = member.shape[1]
    absorbed = jnp.concatenate([result_ref[...], jnp.zeros((LANES - LEV, slots), f32)], axis=0)
    high = absorbed.astype(bf16)
    low = (absorbed - high.astype(f32)).astype(bf16)
    part_ref[...] = (mxu(member, high, NT) + mxu(member, low, NT)).reshape(2, chips, LANES)

    copy = remote(part_ref.at[1 - core], other_ref, send_b, recv_b, 1, sibling)
    copy.start()
    copy.wait()
    strip_ref[...] = (part_ref[core] + other_ref[...]).reshape(chips, 1, LANES)
    copies = [
        remote(strip_ref.at[lax.div(device[0], 2) * n_lat + device[1]], last_ref.at[n], send_c, recv_c, n, device)
        for n, device in enumerate(peers)
    ]
    for copy in copies:
        copy.start()
    for copy in copies:
        copy.wait()
    total = strip_ref[chip] + jnp.sum(last_ref[...], axis=0)
    mean_ref[...] = total[:, :LEV] * (1.0 / LANES)


def columns_absorbed(features, cosine, albedo, sunlit, column_map, swap_list, gas_table, asymmetry, solar):
    anywhere = pl.BlockSpec(memory_space=pl.ANY)
    vmem = pl.BlockSpec(memory_space=pltpu.VMEM)
    f32, bf16, i32 = jnp.float32, jnp.bfloat16, jnp.int32
    chips = lax.axis_size("lon") * lax.axis_size("lat") // 2
    dma = pltpu.SemaphoreType.DMA
    return pl.pallas_call(
        column_kernel,
        out_shape=(pltpu.VMEM((LEV, 2 * LANES), f32), pltpu.VMEM((1, LEV), f32)),
        in_specs=[anywhere] * 9,
        out_specs=(vmem, vmem),
        scratch_shapes=[
            pltpu.VMEM((2 * LANES, LEV * NF), bf16),
            pltpu.VMEM((2 * LANES,), bf16),
            pltpu.VMEM((2, 2 * LANES), bf16),
            pltpu.VMEM((1, 2 * LANES), i32),
            pltpu.VMEM((1, 2 * LANES), i32),
            pltpu.VMEM((NF, 2 * G), bf16),
            pltpu.VMEM((1, G), f32),
            pltpu.VMEM((1, G), f32),
            pltpu.VMEM((1, LANES // 2), i32),
            pltpu.VMEM((KINDS * G, LANES), bf16),
            pltpu.VMEM((3, G, LANES), f32),
            pltpu.VMEM((G, LANES), f32),
            pltpu.VMEM((KINDS * G, 2 * LANES), f32),
            pltpu.VMEM((KINDS * G, 2 * LANES), f32),
            pltpu.VMEM((KINDS * G, 2 * LANES), f32),
            pltpu.VMEM((KINDS * G, 2 * LANES), f32),
            pltpu.VMEM((KINDS * G, 2 * LANES), f32),
            pltpu.VMEM((KINDS * G, 2 * LANES), f32),
            pltpu.VMEM((KINDS * G, 2 * LANES), f32),
            pltpu.VMEM((KINDS * G, 2 * LANES), f32),
            pltpu.VMEM((4, G, LANES), f32),
            pltpu.VMEM((LEV, G, LANES), f32),
            pltpu.VMEM((LEV, G, LANES), f32),
            pltpu.VMEM((LEV, G, LANES), f32),
            pltpu.VMEM((LEV, SUB, LANES), f32),
            pltpu.VMEM((LEV + SUB, LANES), f32),
            pltpu.VMEM((1, 2 * LANES), f32),
            pltpu.VMEM((2 * chips, 2 * LANES), bf16),
            pltpu.VMEM((1, 1, LANES), f32),
            pltpu.VMEM((2, chips, 1, LANES), f32),
            pltpu.VMEM((2, chips, LANES), f32),
            pltpu.VMEM((chips, LANES), f32),
            pltpu.VMEM((chips, 1, LANES), f32),
            pltpu.VMEM((chips - 1, 1, LANES), f32),
            dma((8,)), dma((2,)), dma((chips,)), dma((chips,)), dma((2,)), dma((2,)), dma((chips,)), dma((chips,)),
        ],
        compiler_params=pltpu.CompilerParams(collective_id=0, has_side_effects=True, vmem_limit_bytes=60 * 1024 * 1024),
        cost_estimate=pl.CostEstimate(flops=200_000_000, bytes_accessed=2_200_000, transcendentals=10_000_000),
    )(features, cosine, albedo, sunlit[None], column_map[None], gas_table, asymmetry[None], solar[None], swap_list[None])

def body(
    features, cosine_zenith, albedo, sunlit, column_map, swap_list, gas_table, asymmetry, solar_source
):
    return columns_absorbed(
        features, cosine_zenith, albedo, sunlit, column_map, swap_list, gas_table, asymmetry, solar_source
    )


def solution(mesh):
    both = ("lon", "lat")
    in_specs = (
        P(both, None), P(both), P(None, both), P(both), P(both), P(both), P(), P(), P(),
    )
    out_specs = (P(None, both), P(both, None))
    return jax.shard_map(body, mesh=mesh, in_specs=in_specs, out_specs=out_specs, check_vma=False)
```

```python
import functools
import jax
import jax.numpy as jnp
from jax import lax
from jax.sharding import PartitionSpec as P
from jax.experimental import pallas as pl
from jax.experimental.pallas import tpu as pltpu

LEV = 64
NF = 64
G = 112
LANES = 128
SUB = 8
GB = G // SUB
PAIRS = LEV // 2
KINDS = 2
LOG2E = 1.4426950408889634
NT = (((1,), (1,)), ((), ()))
NN = (((1,), (0,)), ((), ()))


def recip(x):
    return pl.reciprocal(x, approx=True)


def mxu(a, b, dims):
    return lax.dot_general(a, b, dims, preferred_element_type=jnp.float32)


def column_kernel(
    feat_hbm, cosine_hbm, albedo_hbm, sunlit_hbm, map_hbm, gas_hbm, asym_hbm, solar_hbm, swap_hbm,
    result_ref, mean_ref,
    feat_ref, cosine_ref, albedo_ref, sunlit_ref, map_ref, gas_ref, asym_ref, solar_ref, swap_ref,
    weight_ref, const_ref, solar_rows_ref, depth_0, depth_1, depth_2, depth_3, depth_4, depth_5, depth_6, depth_7,
    state_ref, gain_ref, add_ref, admit_ref, down_ref, net_ref,
    wide_ref, member_ref, own_ref, mask_ref, part_ref, other_ref, strip_ref, last_ref,
    small_sem, feat_sem, send_a, recv_a, send_b, recv_b, send_c, recv_c,
):
    f32 = jnp.float32
    bf16 = jnp.bfloat16
    head = 12 * LANES
    pieces = ((0, 0, head), (0, head, LEV * NF - head), (LANES, 0, LEV * NF))
    chunks = [
        pltpu.make_async_copy(
            feat_hbm.at[pl.ds(top, LANES), pl.ds(left_edge, width)],
            feat_ref.at[pl.ds(top, LANES), pl.ds(left_edge, width)],
            feat_sem.at[n],
        )
        for n, (top, left_edge, width) in enumerate(pieces)
    ]
    small = [
        pltpu.make_async_copy(src, dst, small_sem.at[n])
        for n, (src, dst) in enumerate(
            (
                (sunlit_hbm, sunlit_ref), (map_hbm, map_ref), (cosine_hbm, cosine_ref),
                (albedo_hbm, albedo_ref), (gas_hbm, gas_ref), (asym_hbm, asym_ref), (solar_hbm, solar_ref),
                (swap_hbm, swap_ref),
            )
        )
    ]
    for copy in small:
        copy.start()
    for copy in chunks:
        copy.start()

    n_lon, n_lat = lax.axis_size("lon"), lax.axis_size("lat")
    lon, lat = lax.axis_index("lon"), lax.axis_index("lat")
    groups = n_lon * n_lat
    chips = groups // 2
    core = lax.rem(lon, 2)
    chip = lax.div(lon, 2) * n_lat + lat
    mesh_ids = pl.DeviceIdType.MESH
    sibling = (lon + 1 - 2 * core, lat)
    n_x, n_z = n_lon // 4, n_lat // 2
    steps = [
        (dx, high, dz, low_bit)
        for dx in range(n_x) for high in range(2) for dz in range(n_z) for low_bit in range(2)
        if dx or high or dz or low_bit
    ]
    steps.sort(key=lambda d: -(min(d[0], n_x - d[0]) + min(d[2], n_z - d[2]) + (1 if d[3] else 2 * d[1])))
    x, y_high = lax.div(lon, 4), lax.rem(lax.div(lon, 2), 2)
    z, y_low = lax.div(lat, 2), lax.rem(lat, 2)
    peers = [
        (
            lax.rem(x + dx, n_x) * 4 + lax.rem(y_high + high, 2) * 2 + core,
            lax.rem(z + dz, n_z) * 2 + lax.rem(y_low + low_bit, 2),
        )
        for dx, high, dz, low_bit in steps
    ]
    barrier = pltpu.get_barrier_semaphore()
    for device in [sibling] + peers:
        pl.semaphore_signal(barrier, inc=1, device_id=device, device_id_type=mesh_ids)

    def remote(src, dst, sends, recvs, n, device):
        return pltpu.make_async_remote_copy(
            src_ref=src, dst_ref=dst, send_sem=sends.at[n], recv_sem=recvs.at[n],
            device_id=device, device_id_type=mesh_ids,
        )

    mask_copies = [
        remote(own_ref.at[0], mask_ref.at[core, chip], send_a, recv_a, n, device)
        for n, device in enumerate(peers)
    ]
    mask_pair = remote(mask_ref.at[core], mask_ref.at[core], send_b, recv_b, 0, sibling)

    for copy in small:
        copy.wait()

    listed = jnp.broadcast_to(swap_ref[...].astype(f32), (LANES, LANES // 2)).T
    lane_no = lax.broadcasted_iota(jnp.int32, (LANES // 2, LANES), 1).astype(f32)
    own_ref[0] = jnp.max(jnp.where(listed == lane_no, 1.0, 0.0), axis=0, keepdims=True)

    wide_ref[...] = jnp.reshape(cosine_ref[...].astype(f32), (1, 2 * LANES))
    table = gas_ref[...]
    stacked = jnp.concatenate([table, table], axis=0)
    row = lax.broadcasted_iota(jnp.int32, (2 * G, 2 * G), 0)
    col = lax.broadcasted_iota(jnp.int32, (2 * G, 2 * G), 1)
    turned = mxu(jnp.where(row == col, 1.0, 0.0).astype(bf16), stacked, NT)

    def to_rows(line):
        return jnp.broadcast_to(line, (LANES, G)).T

    asym = to_rows(asym_ref[...])
    solar_rows_ref[...] = to_rows(solar_ref[...])
    absorb = turned[:G]
    scatter = turned[G:]
    first = lax.broadcasted_iota(jnp.int32, (G, LANES), 1) < NF
    weight_ref[:G, :] = jnp.where(first, 2.0 * absorb, 2.0 * scatter).astype(bf16)
    weight_ref[G:, :] = jnp.where(first, 0.0, 2.0 * scatter).astype(bf16)
    const_ref[0] = 0.245 * (1.0 + 3.0 * asym)
    const_ref[1] = 0.98 * (0.5 - 0.25 * asym)
    const_ref[2] = 0.98 * (0.5 + 0.25 * asym)

    low_lanes = lax.broadcasted_iota(jnp.int32, (LANES, LANES), 1) < NF

    def one_block(block, carry):
        @pl.when(block == 0)
        def _():
            chunks[0].wait()

        @pl.when(block == 1)
        def _():
            chunks[2].wait()

        lanes = pl.ds(pl.multiple_of(block * LANES, LANES), LANES)
        cosine = wide_ref[:, lanes]
        slant = jnp.broadcast_to((-0.5 * LOG2E) / cosine, (SUB, LANES))
        alb_dir = jnp.broadcast_to(albedo_ref[0:1, lanes].astype(f32), (SUB, LANES))
        alb_dif = jnp.broadcast_to(albedo_ref[1:2, lanes].astype(f32), (SUB, LANES))
        state_ref[0] = solar_rows_ref[...] * (cosine * sunlit_ref[:, lanes].astype(f32))
        state_ref[1] = jnp.ones((G, LANES), f32)
        state_ref[2] = jnp.zeros((G, LANES), f32)
        state_ref[3] = jnp.zeros((G, LANES), f32)

        def optical(pair, depth, guard=None):
            chunk = feat_ref[lanes, pl.ds(pl.multiple_of(pair * LANES, LANES), LANES)]
            if guard is not None:
                chunk = chunk + guard
            turn = chunk.T
            both = jnp.concatenate(
                [
                    jnp.concatenate([turn[:NF], turn[:NF]], axis=0),
                    jnp.concatenate([turn[NF:], turn[NF:]], axis=0),
                ],
                axis=1,
            )
            depth[...] = mxu(weight_ref[...], both, NN)

        def one_pair(pair, depth):
            totals = [jnp.zeros((SUB, LANES), f32) for _ in range(2)]
            for g in range(GB):
                rows = pl.ds(g * SUB, SUB)
                direct, admit, source, left = (state_ref[n, rows, :] for n in range(4))
                slope, to_up, to_dn = (const_ref[n, rows, :] for n in range(3))
                for odd in range(2):
                    layer = 2 * pair + odd
                    tau, ray = (
                        depth[n * G + g * SUB : n * G + (g + 1) * SUB, odd * LANES : (odd + 1) * LANES]
                        for n in range(KINDS)
                    )
                    t_one = tau - 0.98 * ray
                    t_two = tau - slope * ray
                    root = lax.rsqrt(t_two)
                    first_root = t_one * lax.rsqrt(t_one)
                    x = first_root * (t_two * root)
                    sigma = first_root * root
                    th = jnp.tanh(x)
                    e = jnp.exp2(x * (-LOG2E))
                    sech = e + e * th
                    below = direct * jnp.exp2(tau * slant)
                    lost = (direct - below) * recip(tau) * ray
                    up = to_up * lost
                    dn = to_dn * lost
                    jump = up - left
                    totals[odd] = totals[odd] + (source + direct)
                    inner = source + up - admit * jump
                    z = recip(sigma + admit * th)
                    zs = z * sigma
                    gain = sech * zs
                    gain_ref[layer, rows, :] = gain
                    add_ref[layer, rows, :] = (th * z) * inner + jump
                    admit_ref[layer, rows, :] = admit
                    admit = (admit + sigma * th) * zs
                    source = gain * inner + dn
                    direct = below
                    left = dn
                for n, value in enumerate((direct, admit, source, left)):
                    state_ref[n, rows, :] = value
            for odd in range(2):
                down_ref[2 * pair + odd] = totals[odd]
            return jnp.minimum(th[0:1], 0.0).astype(bf16)

        optical(0, depth_0)
        optical(1, depth_1)
        optical(2, depth_2)
        optical(3, depth_3)

        def down(step, inner_carry):
            @pl.when((block == 0) & (step == 1))
            def _():
                chunks[1].wait()

            @pl.when((block == 0) & (step == PAIRS // 8 - 1))
            def _():
                pl.semaphore_wait(barrier, chips)
                mask_ref[core, chip] = own_ref[0]
                for copy in mask_copies:
                    copy.start()

            @pl.when((block == 1) & (step == PAIRS // 8 - 1))
            def _():
                for copy in mask_copies:
                    copy.wait()
                mask_pair.start()

            guard = None
            next_guard = one_pair(8 * step + 0, depth_0)
            optical(8 * step + 4, depth_4, guard)
            guard = next_guard
            next_guard = one_pair(8 * step + 1, depth_1)
            optical(8 * step + 5, depth_5, guard)
            guard = next_guard
            next_guard = one_pair(8 * step + 2, depth_2)
            optical(8 * step + 6, depth_6, guard)
            guard = next_guard
            next_guard = one_pair(8 * step + 3, depth_3)
            optical(8 * step + 7, depth_7, guard)
            guard = next_guard
            next_guard = one_pair(8 * step + 4, depth_4)
            optical(jnp.minimum(8 * step + 8, PAIRS - 1), depth_0, guard)
            guard = next_guard
            next_guard = one_pair(8 * step + 5, depth_5)
            optical(jnp.minimum(8 * step + 9, PAIRS - 1), depth_1, guard)
            guard = next_guard
            next_guard = one_pair(8 * step + 6, depth_6)
            optical(jnp.minimum(8 * step + 10, PAIRS - 1), depth_2, guard)
            guard = next_guard
            next_guard = one_pair(8 * step + 7, depth_7)
            optical(jnp.minimum(8 * step + 11, PAIRS - 1), depth_3, guard)
            guard = next_guard
            return inner_carry

        lax.fori_loop(0, PAIRS // 8, down, 0)

        @pl.when(block == 1)
        def _():
            mask_pair.wait()

            place = map_ref[...]
            home = lax.shift_right_arithmetic(place, 7)
            home_core = lax.rem(lax.div(home, n_lat), 2)
            home_chip = lax.div(home, 2 * n_lat) * n_lat + lax.rem(home, n_lat)
            away_chip = jnp.where(home_chip >= chips // 2, home_chip - chips // 2, home_chip + chips // 2)
            slot = place & (LANES - 1)
            slots = place.shape[1]
            group_row = lax.broadcasted_iota(jnp.int32, (groups, slots), 0)
            at_home = jnp.where(home_core * chips + home_chip == group_row, 1.0, 0.0).astype(bf16)
            at_slot = jnp.where(slot == lax.broadcasted_iota(jnp.int32, (LANES, slots), 0), 1.0, 0.0)
            masks = mask_ref[...].reshape(groups, LANES)
            listed_at = mxu(masks.T.astype(bf16), at_home, NN)
            moved = jnp.sum(listed_at * at_slot, axis=0, keepdims=True)
            held = home_core * chips + jnp.where(moved > 0.5, away_chip, home_chip)
            held = jnp.where(place < 0, -1, held)
            member_ref[...] = jnp.where(held == group_row, 1.0, 0.0).astype(bf16)

        fluxes = []
        total = jnp.zeros((SUB, LANES), f32)
        for g in range(GB):
            rows = pl.ds(g * SUB, SUB)
            direct, admit, source, left = (state_ref[n, rows, :] for n in range(4))
            over = source * (1.0 + alb_dif) + 2.0 * alb_dir * direct - left * (1.0 - alb_dif)
            flux = over / ((1.0 - alb_dif) + admit * (1.0 + alb_dif))
            total = total + (direct + source - admit * flux)
            fluxes.append(flux)
        net_ref[LEV : LEV + 1, :] = jnp.sum(total, axis=0, keepdims=True)

        def upward(step, fluxes):
            for odd in range(4):
                layer = LEV - 1 - 4 * step - odd
                total = down_ref[layer]
                out = []
                for g in range(GB):
                    rows = pl.ds(g * SUB, SUB)
                    flux = gain_ref[layer, rows, :] * fluxes[g] + add_ref[layer, rows, :]
                    total = total - admit_ref[layer, rows, :] * flux
                    out.append(flux)
                fluxes = tuple(out)
                net_ref[pl.ds(layer, 1), :] = jnp.sum(total, axis=0, keepdims=True)
            return fluxes

        lax.fori_loop(0, LEV // 4, upward, tuple(fluxes))
        live = map_ref[:, lanes] >= 0
        result_ref[:, lanes] = jnp.where(live, net_ref[0:LEV, :] - net_ref[1 : LEV + 1, :], 0.0)
        return carry

    lax.fori_loop(0, 2, one_block, 0)

    member = member_ref[...]
    slots = member.shape[1]
    absorbed = jnp.concatenate([result_ref[...], jnp.zeros((LANES - LEV, slots), f32)], axis=0)
    high = absorbed.astype(bf16)
    low = (absorbed - high.astype(f32)).astype(bf16)
    part_ref[...] = (mxu(member, high, NT) + mxu(member, low, NT)).reshape(2, chips, LANES)

    copy = remote(part_ref.at[1 - core], other_ref, send_b, recv_b, 1, sibling)
    copy.start()
    copy.wait()
    strip_ref[...] = (part_ref[core] + other_ref[...]).reshape(chips, 1, LANES)
    copies = [
        remote(strip_ref.at[lax.div(device[0], 2) * n_lat + device[1]], last_ref.at[n], send_c, recv_c, n, device)
        for n, device in enumerate(peers)
    ]
    for copy in copies:
        copy.start()
    for copy in copies:
        copy.wait()
    total = strip_ref[chip] + jnp.sum(last_ref[...], axis=0)
    mean_ref[...] = total[:, :LEV] * (1.0 / LANES)


def columns_absorbed(features, cosine, albedo, sunlit, column_map, swap_list, gas_table, asymmetry, solar):
    anywhere = pl.BlockSpec(memory_space=pl.ANY)
    vmem = pl.BlockSpec(memory_space=pltpu.VMEM)
    f32, bf16, i32 = jnp.float32, jnp.bfloat16, jnp.int32
    chips = lax.axis_size("lon") * lax.axis_size("lat") // 2
    dma = pltpu.SemaphoreType.DMA
    return pl.pallas_call(
        column_kernel,
        out_shape=(pltpu.VMEM((LEV, 2 * LANES), f32), pltpu.VMEM((1, LEV), f32)),
        in_specs=[anywhere] * 9,
        out_specs=(vmem, vmem),
        scratch_shapes=[
            pltpu.VMEM((2 * LANES, LEV * NF), bf16),
            pltpu.VMEM((2 * LANES,), bf16),
            pltpu.VMEM((2, 2 * LANES), bf16),
            pltpu.VMEM((1, 2 * LANES), i32),
            pltpu.VMEM((1, 2 * LANES), i32),
            pltpu.VMEM((NF, 2 * G), bf16),
            pltpu.VMEM((1, G), f32),
            pltpu.VMEM((1, G), f32),
            pltpu.VMEM((1, LANES // 2), i32),
            pltpu.VMEM((KINDS * G, LANES), bf16),
            pltpu.VMEM((3, G, LANES), f32),
            pltpu.VMEM((G, LANES), f32),
            pltpu.VMEM((KINDS * G, 2 * LANES), f32),
            pltpu.VMEM((KINDS * G, 2 * LANES), f32),
            pltpu.VMEM((KINDS * G, 2 * LANES), f32),
            pltpu.VMEM((KINDS * G, 2 * LANES), f32),
            pltpu.VMEM((KINDS * G, 2 * LANES), f32),
            pltpu.VMEM((KINDS * G, 2 * LANES), f32),
            pltpu.VMEM((KINDS * G, 2 * LANES), f32),
            pltpu.VMEM((KINDS * G, 2 * LANES), f32),
            pltpu.VMEM((4, G, LANES), f32),
            pltpu.VMEM((LEV, G, LANES), f32),
            pltpu.VMEM((LEV, G, LANES), f32),
            pltpu.VMEM((LEV, G, LANES), f32),
            pltpu.VMEM((LEV, SUB, LANES), f32),
            pltpu.VMEM((LEV + SUB, LANES), f32),
            pltpu.VMEM((1, 2 * LANES), f32),
            pltpu.VMEM((2 * chips, 2 * LANES), bf16),
            pltpu.VMEM((1, 1, LANES), f32),
            pltpu.VMEM((2, chips, 1, LANES), f32),
            pltpu.VMEM((2, chips, LANES), f32),
            pltpu.VMEM((chips, LANES), f32),
            pltpu.VMEM((chips, 1, LANES), f32),
            pltpu.VMEM((chips - 1, 1, LANES), f32),
            dma((8,)), dma((3,)), dma((chips,)), dma((chips,)), dma((2,)), dma((2,)), dma((chips,)), dma((chips,)),
        ],
        compiler_params=pltpu.CompilerParams(collective_id=0, has_side_effects=True, vmem_limit_bytes=60 * 1024 * 1024),
        cost_estimate=pl.CostEstimate(flops=200_000_000, bytes_accessed=2_200_000, transcendentals=10_000_000),
    )(features, cosine, albedo, sunlit[None], column_map[None], gas_table, asymmetry[None], solar[None], swap_list[None])

def body(
    features, cosine_zenith, albedo, sunlit, column_map, swap_list, gas_table, asymmetry, solar_source
):
    return columns_absorbed(
        features, cosine_zenith, albedo, sunlit, column_map, swap_list, gas_table, asymmetry, solar_source
    )


def solution(mesh):
    both = ("lon", "lat")
    in_specs = (
        P(both, None), P(both), P(None, both), P(both), P(both), P(both), P(), P(), P(),
    )
    out_specs = (P(None, both), P(both, None))
    return jax.shard_map(body, mesh=mesh, in_specs=in_specs, out_specs=out_specs, check_vma=False)
```
